32 devices in a mesh: seq: 8 (over y, x, core), fsdp: 4 (over z).
Axes of the slice: x: 2, y: 2, z: 4, core: 2. Of those that a mesh axis runs over, the one named last changes fastest.
Arguments:
- normed_block_input: bfloat16 [4, 1024, 8192], P('fsdp', 'seq'), may hold values from -6 to 6
- stored_rotated_queries: bfloat16 [4, 1024, 4096], P('fsdp', 'seq'), may hold values from -640 to 640
- stored_rotated_keys: bfloat16 [4, 1024, 512], P('fsdp', 'seq'), may hold values from -4 to 4
- attention_output_gradient: bfloat16 [4, 1024, 4096], P('fsdp', 'seq'), may hold values from -6 to 6
- frozen_value_weight: bfloat16 [8192, 512], P('fsdp'), may hold values from -0.0625 to 0.0625
- adapter_down_weight: bfloat16 [16, 8192], replicated, may hold values from -0.0625 to 0.0625
- adapter_up_weight: bfloat16 [16, 512], replicated, may hold values from -1.5 to 1.5
- packed_document_lengths: int32 [4, 8], P('fsdp'), may hold values from 1 to 256, 1024 in all within a row
Outputs:
- input_gradient: bfloat16 [4, 1024, 8192], P('fsdp', 'seq')
- rotated_query_gradient: bfloat16 [4, 1024, 4096], P('fsdp', 'seq')
- rotated_key_gradient: bfloat16 [4, 1024, 512], P('fsdp', 'seq')
- adapter_down_gradient: float32 [16, 8192], replicated
- adapter_up_gradient: float32 [16, 512], replicated
The draws below stay inside these ranges and needn't reach their ends.
Inputs may be any that keep to these rules, and one draw needn't show every extreme that they name: `packed_document_lengths`: row g holds, in order, the lengths of the 8 documents packed into sequence g; they sum to 1024, and in every row the longest has exactly 256 tokens.
All inputs are finite; a program needn't handle non-finite values.
Results may differ from the reference program's by a relative error of at most 0.0065.
Values may be sent and summed in bfloat16 or wider, within the bound.
No kernel may reach another device: no remote copies, remote signals or barrier semaphores. Data moves between devices by JAX's collectives and lax.ppermute only.
A program may use at most 128 MiB of HBM per device.

```python
import math
import jax
import jax.numpy as jnp
import numpy as np
from jax import lax

MODEL_DIMENSION = 8192
HEAD_FEATURES = 128
QUERY_HEADS = 32
KEY_VALUE_HEADS = 4
ADAPTER_RANK = 16
DOCS = 8
SEQUENCE_TOKENS = 1024
TOKEN_COUNT = 4096
DOC_MOST = 256
CQ = 4096
KEY_VALUE_WIDTH = 512
N_FSDP = 4


def paired_draw(key):
    base_key = jax.random.fold_in(key, 9173)
    key_query, random_key_split = jax.random.split(base_key, 2)
    queries = jnp.clip(jax.random.normal(key_query, (N_FSDP, SEQUENCE_TOKENS, QUERY_HEADS, HEAD_FEATURES), jnp.float32), -4.0, 4.0)
    complete_keys = jnp.clip(jax.random.normal(random_key_split, (N_FSDP, SEQUENCE_TOKENS, KEY_VALUE_HEADS, HEAD_FEATURES), jnp.float32), -4.0, 4.0)
    return (queries, complete_keys)


def draw_stored_rotated_queries(key, part):
    queries, complete_keys = paired_draw(key)
    return queries.reshape(N_FSDP, SEQUENCE_TOKENS, QUERY_HEADS * HEAD_FEATURES).astype(jnp.bfloat16)


def draw_stored_rotated_keys(key, part):
    queries, complete_keys = paired_draw(key)
    return complete_keys.reshape(N_FSDP, SEQUENCE_TOKENS, KEY_VALUE_HEADS * HEAD_FEATURES).astype(jnp.bfloat16)


def steps_of(key, dims, pieces, smallest, top_value):
    factor_of = 1.0
    for dim, parts in pieces:
        steps = jax.random.uniform(jax.random.fold_in(jax.random.fold_in(key, 6), dim), (parts,), jnp.float32, smallest / len(pieces), top_value / len(pieces))
        factor_of = factor_of * jnp.repeat(jnp.exp(steps), dims[dim] // parts).reshape((-1,) + (1,) * (len(dims) - 1 - dim))
    return factor_of


def split_up(amount, total, bound, slope):
    weights = [(1 << 20) // math.isqrt(standing ** slope) + 1 for standing in range(2, amount + 1)]
    spare, holding = total - bound - (amount - 1), [1] * (amount - 1)
    while spare > 0:
        free = [i for i in range(amount - 1) if holding[i] < bound]
        mass, remaining = sum([weights[i] for i in free]), spare
        for i in free:
            addition = min(bound - holding[i], max(1, remaining * weights[i] // mass), spare)
            holding[i] = holding[i] + addition
            spare = spare - addition
    return np.array([bound] + holding)


def uneven(stream_key, count, total, bound, skew):
    if count == 2:
        one = jax.random.randint(stream_key, (), max(1, total - bound), min(bound, total - 1) + 1)
        return jnp.stack([one, total - one])
    sizes = jnp.asarray(split_up(count, total, bound, skew), jnp.int32)
    twos = (count - 1) // 2
    giver, sink = sizes[1:1 + 2 * twos:2], sizes[2:2 + 2 * twos:2]
    slack = jnp.minimum(giver - 1, bound - sink)
    shifted = jax.random.randint(jax.random.fold_in(stream_key, 1), (twos,), 0, 1 << 20) % (slack + 1)
    sizes = sizes.at[1:1 + 2 * twos:2].set(giver - shifted).at[2:2 + 2 * twos:2].set(sink + shifted)
    return sizes[jax.random.permutation(jax.random.fold_in(stream_key, 2), count)]


def centred(key, dims, deviation, bound, cuts=(), kind=jnp.bfloat16):
    values = deviation * jax.random.normal(key, dims, jnp.float32)
    if cuts:
        values = values * steps_of(key, dims, cuts, -0.22, 0.18)
    return jnp.clip(values, -bound, bound).astype(kind)


def setup_inputs(seed: int = 0) -> dict:
    arg_keys = jax.random.split(jax.random.key(seed), 9)
    return {
        "normed_block_input": centred(arg_keys[0], (N_FSDP, SEQUENCE_TOKENS, MODEL_DIMENSION), 1.0, 6.0, ((0, 4), (1, 8))),
        "stored_rotated_queries": draw_stored_rotated_queries(jax.random.fold_in(arg_keys[8], 71), 0),
        "stored_rotated_keys": draw_stored_rotated_keys(jax.random.fold_in(arg_keys[8], 71), 0),
        "attention_output_gradient": centred(arg_keys[3], (N_FSDP, SEQUENCE_TOKENS, CQ), 1.0, 6.0, ((0, 4), (1, 8))),
        "frozen_value_weight": centred(arg_keys[4], (MODEL_DIMENSION, KEY_VALUE_WIDTH), MODEL_DIMENSION ** -0.5, 0.0625, ((0, 4),)),
        "adapter_down_weight": centred(arg_keys[5], (ADAPTER_RANK, MODEL_DIMENSION), MODEL_DIMENSION ** -0.5, 0.0625),
        "adapter_up_weight": centred(arg_keys[6], (ADAPTER_RANK, KEY_VALUE_WIDTH), ADAPTER_RANK ** -0.5, 1.5),
        "packed_document_lengths": jax.vmap(lambda own: uneven(own, DOCS, SEQUENCE_TOKENS, DOC_MOST, 2))(jax.random.split(arg_keys[7], N_FSDP)).reshape((N_FSDP, DOCS)).astype(jnp.int32),
    }


ADAPTER_SCALE = 2.0
NEG_FILL = -1e30


def segment_ids(lengths_row, length):
    bounds = jnp.cumsum(lengths_row)
    places = jnp.arange(length, dtype=jnp.int32)
    return jnp.sum((places[:, None] >= bounds[None, :]).astype(jnp.int32), axis=1)


def head_backward(query_head, key_head, value_head, grad_head, allowed):
    inverse = HEAD_FEATURES ** -0.5
    scores = jnp.dot(query_head, key_head.T, preferred_element_type=jnp.float32) * inverse
    scores = jnp.where(allowed, scores, NEG_FILL)
    row_peak = jnp.max(scores, axis=1, keepdims=True)
    weights = jnp.exp(scores - row_peak)
    probs_full = weights / jnp.sum(weights, axis=1, keepdims=True)
    probs_low = probs_full.astype(jnp.bfloat16)
    grad_probs = jnp.dot(grad_head, value_head.T, preferred_element_type=jnp.float32)
    row_delta = jnp.sum(probs_full * grad_probs, axis=1, keepdims=True)
    grad_scores = (probs_full * (grad_probs - row_delta)).astype(jnp.bfloat16)
    grad_query = jnp.dot(grad_scores, key_head, preferred_element_type=jnp.float32) * inverse
    key_gradient_rows = jnp.dot(grad_scores.T, query_head, preferred_element_type=jnp.float32) * inverse
    value_gradient_rows = jnp.dot(probs_low.T, grad_head, preferred_element_type=jnp.float32)
    return grad_query, key_gradient_rows, value_gradient_rows


def group_backward(group_item):
    query_rows, key_token_rows, value_token_rows, grad_rows, lengths_row = group_item
    queries_per_group = QUERY_HEADS // KEY_VALUE_HEADS
    segments = segment_ids(lengths_row, SEQUENCE_TOKENS)
    places = jnp.arange(SEQUENCE_TOKENS, dtype=jnp.int32)
    allowed = (places[None, :] <= places[:, None]) & (segments[:, None] == segments[None, :])
    query_heads = query_rows.reshape(SEQUENCE_TOKENS, QUERY_HEADS, HEAD_FEATURES).transpose(1, 0, 2)
    grad_heads = grad_rows.reshape(SEQUENCE_TOKENS, QUERY_HEADS, HEAD_FEATURES).transpose(1, 0, 2)
    key_head_split = jnp.repeat(key_token_rows.reshape(SEQUENCE_TOKENS, KEY_VALUE_HEADS, HEAD_FEATURES).transpose(1, 0, 2), queries_per_group, axis=0)
    value_head_split = jnp.repeat(value_token_rows.reshape(SEQUENCE_TOKENS, KEY_VALUE_HEADS, HEAD_FEATURES).transpose(1, 0, 2), queries_per_group, axis=0)

    def one_head(head_item):
        return head_backward(head_item[0], head_item[1], head_item[2], head_item[3], allowed)

    grad_query, key_gradient_rows, value_gradient_rows = lax.map(one_head, (query_heads, key_head_split, value_head_split, grad_heads))
    grad_query = grad_query.transpose(1, 0, 2).reshape(SEQUENCE_TOKENS, QUERY_HEADS * HEAD_FEATURES)
    key_gradient_rows = key_gradient_rows.reshape(KEY_VALUE_HEADS, queries_per_group, SEQUENCE_TOKENS, HEAD_FEATURES).sum(axis=1).transpose(1, 0, 2).reshape(SEQUENCE_TOKENS, KEY_VALUE_HEADS * HEAD_FEATURES)
    value_gradient_rows = value_gradient_rows.reshape(KEY_VALUE_HEADS, queries_per_group, SEQUENCE_TOKENS, HEAD_FEATURES).sum(axis=1).transpose(1, 0, 2).reshape(SEQUENCE_TOKENS, KEY_VALUE_HEADS * HEAD_FEATURES)
    return grad_query, key_gradient_rows, value_gradient_rows


def reference(normed_block_input, stored_rotated_queries, stored_rotated_keys, attention_output_gradient, frozen_value_weight, adapter_down_weight, adapter_up_weight, packed_document_lengths):
    hidden_activations = normed_block_input.reshape(TOKEN_COUNT, MODEL_DIMENSION)
    adapter_projection = lax.dot_general(hidden_activations, adapter_down_weight, (((1,), (1,)), ((), ())), preferred_element_type=jnp.float32)
    up_widened = adapter_up_weight.astype(jnp.float32)
    adapter_values = (jnp.dot(hidden_activations, frozen_value_weight, preferred_element_type=jnp.float32)
                  + ADAPTER_SCALE * jnp.dot(adapter_projection, up_widened, precision=lax.Precision.HIGHEST)).astype(jnp.bfloat16)
    adapter_values = adapter_values.reshape(N_FSDP, SEQUENCE_TOKENS, KEY_VALUE_HEADS * HEAD_FEATURES)
    grad_query, key_gradient_rows, value_gradient_rows = lax.map(group_backward, (stored_rotated_queries, stored_rotated_keys, adapter_values, attention_output_gradient, packed_document_lengths))
    value_gradient_matrix = value_gradient_rows.reshape(TOKEN_COUNT, KEY_VALUE_HEADS * HEAD_FEATURES)
    value_grad_low = value_gradient_matrix.astype(jnp.bfloat16)
    adapter_rank_gradient = ADAPTER_SCALE * lax.dot_general(value_gradient_matrix, up_widened, (((1,), (1,)), ((), ())), precision=lax.Precision.HIGHEST)
    reduced_rank_gradient = adapter_rank_gradient.astype(jnp.bfloat16)
    input_gradient = (lax.dot_general(value_grad_low, frozen_value_weight, (((1,), (1,)), ((), ())), preferred_element_type=jnp.float32)
                + jnp.dot(reduced_rank_gradient, adapter_down_weight, preferred_element_type=jnp.float32)).astype(jnp.bfloat16)
    adapter_down_gradient = lax.dot_general(reduced_rank_gradient, hidden_activations, (((0,), (0,)), ((), ())), preferred_element_type=jnp.float32) / TOKEN_COUNT
    adapter_up_gradient = ADAPTER_SCALE * jnp.dot(adapter_projection.T, value_gradient_matrix, precision=lax.Precision.HIGHEST) / TOKEN_COUNT
    return (input_gradient.reshape(N_FSDP, SEQUENCE_TOKENS, MODEL_DIMENSION), grad_query.astype(jnp.bfloat16), key_gradient_rows.astype(jnp.bfloat16),
            adapter_down_gradient, adapter_up_gradient)
```

```python
import math

import jax
import jax.numpy as jnp
import numpy as np
from jax import lax
from jax.experimental import pallas as pl
from jax.experimental.pallas import tpu as pltpu
from jax.sharding import PartitionSpec as P

HEAD_FEATURES = 128
QUERY_HEADS = 32
KEY_VALUE_HEADS = 4
GROUP = QUERY_HEADS // KEY_VALUE_HEADS
ADAPTER_SCALE = 2.0
NEG_FILL = -1e30
INVERSE = HEAD_FEATURES ** (-0.5)
LOG2E = math.log2(math.e)
VMEM_LIMIT = 48 * 1024 * 1024
F32 = jnp.float32
BF16 = jnp.bfloat16


def params():
    return pltpu.CompilerParams(vmem_limit_bytes=VMEM_LIMIT)


def cost(flops, nbytes):
    return pl.CostEstimate(flops=int(flops), bytes_accessed=int(nbytes), transcendentals=0)


def contract_trailing(left, right):
    return lax.dot_general(left, right, (((1,), (1,)), ((), ())), preferred_element_type=F32)


def contract_leading(left, right, precision=None):
    return lax.dot_general(
        left, right, (((0,), (0,)), ((), ())), preferred_element_type=F32, precision=precision
    )


def flip(value, axis, mask):
    size = lax.axis_size(axis)
    choose = mask if callable(mask) else (lambda index: mask)
    return lax.ppermute(value, axis, [(i, i ^ choose(i)) for i in range(size)])


def shift(value, axis, by):
    size = lax.axis_size(axis)
    return lax.ppermute(value, axis, [(i, i + by) for i in range(size) if 0 <= i + by < size])


def turn(value, axis, by):
    size = lax.axis_size(axis)
    return lax.ppermute(value, axis, [(i, (i + by) % size) for i in range(size)])


def pair_rows(ref, index):
    first = ref[:, (2 * index) * HEAD_FEATURES : (2 * index + 1) * HEAD_FEATURES]
    second = ref[:, (2 * index + 1) * HEAD_FEATURES : (2 * index + 2) * HEAD_FEATURES]
    return jnp.concatenate([first, second], axis=0)


def probs_kernel(back, docs, tokens):
    def kernel(info, q_ref, o_ref, *refs):
        key_refs = refs[: back + 1]
        p_ref = refs[back + 1]
        dv_refs = refs[back + 2 : 2 * back + 3]
        bias_ref = refs[2 * back + 3]
        keys = (back + 1) * tokens

        @pl.when(pl.program_id(0) == 0)
        def _():
            here = info[0]
            query_place = here * tokens + lax.broadcasted_iota(jnp.int32, (keys, tokens), 1)
            key_place = (here - back) * tokens + lax.broadcasted_iota(jnp.int32, (keys, tokens), 0)
            opening = jnp.zeros((keys, tokens), jnp.int32)
            bound = jnp.int32(0)
            for doc in range(docs):
                bound = bound + info[1 + doc]
                opening = jnp.where(query_place >= bound, bound, opening)
            allowed = (key_place <= query_place) & (key_place >= opening)
            bias_ref[...] = jnp.where(allowed, 0.0, NEG_FILL)

        key_rows = jnp.concatenate([r[...] for r in key_refs], axis=0)
        total = jnp.zeros((keys, HEAD_FEATURES), F32)
        for pair in range(GROUP // 2):
            scores = contract_trailing(key_rows, pair_rows(q_ref, pair))
            bias = bias_ref[...]
            scores = scores + jnp.concatenate([bias, bias], axis=1)
            peak = jnp.max(scores, axis=0, keepdims=True)
            weights = jnp.exp2((scores - peak) * (INVERSE * LOG2E))
            probs = weights * (1.0 / jnp.sum(weights, axis=0, keepdims=True))
            probs_low = probs.astype(BF16)
            p_ref[0, :, 2 * pair * tokens : 2 * (pair + 1) * tokens] = probs_low
            total = total + jnp.dot(probs_low, pair_rows(o_ref, pair), preferred_element_type=F32)
        for block in range(back + 1):
            rows = total[block * tokens : (block + 1) * tokens]
            dv_refs[block][...] = rows.astype(dv_refs[block].dtype)

    return kernel


def head_blocks(tokens, width):
    return pl.BlockSpec((tokens, width), lambda head, *_: (0, head))


def probs_call(info, q, o, key_blocks):
    back = len(key_blocks) - 1
    tokens = q.shape[0]
    keys = (back + 1) * tokens
    kv = key_blocks[0].shape[1]
    wide = head_blocks(tokens, GROUP * HEAD_FEATURES)
    thin = head_blocks(tokens, HEAD_FEATURES)
    out = pl.pallas_call(
        probs_kernel(back, info.shape[0] - 1, tokens),
        grid_spec=pltpu.PrefetchScalarGridSpec(
            num_scalar_prefetch=1,
            grid=(KEY_VALUE_HEADS,),
            in_specs=[wide, wide] + [thin] * (back + 1),
            out_specs=[pl.BlockSpec((1, keys, GROUP * tokens), lambda head, *_: (head, 0, 0))]
            + [thin] * (back + 1),
            scratch_shapes=[pltpu.VMEM((keys, tokens), F32)],
        ),
        out_shape=[jax.ShapeDtypeStruct((KEY_VALUE_HEADS, keys, GROUP * tokens), BF16)]
        + [jax.ShapeDtypeStruct((tokens, kv), BF16)] * back
        + [jax.ShapeDtypeStruct((tokens, kv), F32)],
        compiler_params=params(),
        cost_estimate=cost(8 * QUERY_HEADS * keys * tokens * HEAD_FEATURES, 8 << 20),
        name="probs",
    )(info, q, o, *key_blocks)
    return out[0], out[1:]


def scores_grad_kernel(back, tokens):
    def kernel(p_ref, q_ref, o_ref, *refs):
        key_refs = refs[: back + 1]
        value_refs = refs[back + 1 : 2 * back + 2]
        dq_ref = refs[2 * back + 2]
        dk_refs = refs[2 * back + 3 :]
        keys = (back + 1) * tokens
        key_rows = jnp.concatenate([r[...] for r in key_refs], axis=0)
        value_rows = jnp.concatenate([r[...] for r in value_refs], axis=0)
        key_columns = key_rows.T
        total = jnp.zeros((keys, HEAD_FEATURES), F32)
        for pair in range(GROUP // 2):
            grad_probs = contract_trailing(value_rows, pair_rows(o_ref, pair))
            probs = p_ref[0, :, 2 * pair * tokens : 2 * (pair + 1) * tokens].astype(F32)
            mass = jnp.sum(probs, axis=0, keepdims=True)
            delta = jnp.sum(probs * grad_probs, axis=0, keepdims=True) / mass
            grad_scores = (probs * (grad_probs - delta)).astype(BF16)
            total = total + jnp.dot(
                grad_scores, pair_rows(q_ref, pair), preferred_element_type=F32
            )
            dq = jnp.dot(key_columns, grad_scores, preferred_element_type=F32) * INVERSE
            dq_ref[:, 2 * pair * HEAD_FEATURES : (2 * pair + 1) * HEAD_FEATURES] = (
                dq[:, :tokens].T.astype(BF16)
            )
            dq_ref[:, (2 * pair + 1) * HEAD_FEATURES : (2 * pair + 2) * HEAD_FEATURES] = (
                dq[:, tokens:].T.astype(BF16)
            )
        for block in range(back + 1):
            rows = total[block * tokens : (block + 1) * tokens] * INVERSE
            dk_refs[block][...] = rows.astype(dk_refs[block].dtype)

    return kernel


def scores_grad_call(probs, q, o, key_blocks, value_blocks):
    back = len(key_blocks) - 1
    tokens = q.shape[0]
    keys = (back + 1) * tokens
    kv = key_blocks[0].shape[1]
    wide = head_blocks(tokens, GROUP * HEAD_FEATURES)
    thin = head_blocks(tokens, HEAD_FEATURES)
    out = pl.pallas_call(
        scores_grad_kernel(back, tokens),
        grid=(KEY_VALUE_HEADS,),
        in_specs=[pl.BlockSpec((1, keys, GROUP * tokens), lambda head: (head, 0, 0)), wide, wide]
        + [thin] * (2 * back + 2),
        out_specs=[wide] + [thin] * (back + 1),
        out_shape=[jax.ShapeDtypeStruct(q.shape, BF16)]
        + [jax.ShapeDtypeStruct((tokens, kv), BF16)] * back
        + [jax.ShapeDtypeStruct((tokens, kv), F32)],
        compiler_params=params(),
        cost_estimate=cost(12 * QUERY_HEADS * keys * tokens * HEAD_FEATURES, 8 << 20),
        name="scores_grad",
    )(probs, q, o, *key_blocks, *value_blocks)
    return out[0], out[1:]


def own_values_kernel(x_ref, own_ref, down_ref, up_ref, w_ref, acc_ref, rank_ref):
    low_rank = contract_trailing(x_ref[...], down_ref[...])
    rank_ref[...] = low_rank
    adapter = jnp.dot(
        low_rank,
        up_ref[...].astype(F32),
        precision=lax.Precision.HIGHEST,
        preferred_element_type=F32,
    )
    acc_ref[...] = ADAPTER_SCALE * adapter + jnp.dot(
        own_ref[...], w_ref[...], preferred_element_type=F32
    )


def own_values_call(place, x, down, up, w):
    tokens, model = x.shape
    rows, kv = w.shape
    rank = down.shape[0]

    def kernel(place_ref, *refs):
        own_values_kernel(*refs)

    def whole(shape):
        return pl.BlockSpec(shape, lambda i, *_: (0, 0))

    return pl.pallas_call(
        kernel,
        grid_spec=pltpu.PrefetchScalarGridSpec(
            num_scalar_prefetch=1,
            grid=(1,),
            in_specs=[
                whole(x.shape),
                pl.BlockSpec((tokens, rows), lambda i, place: (0, place[0])),
                whole(down.shape),
                whole(up.shape),
                whole(w.shape),
            ],
            out_specs=[whole((tokens, kv)), whole((tokens, rank))],
        ),
        out_shape=[
            jax.ShapeDtypeStruct((tokens, kv), F32),
            jax.ShapeDtypeStruct((tokens, rank), F32),
        ],
        compiler_params=params(),
        cost_estimate=cost(2 * tokens * rows * kv * 2, 5 << 20),
        name="own_values",
    )(place, x, x, down, up, w)


def pieces_of(piece_refs, step):
    number = 0
    for ref in piece_refs:
        for j in range(ref.shape[0] // step):
            yield number, ref, j * step
            number += 1


def more_values_call(place, x, acc, pieces, step, last):
    tokens, model = x.shape
    kv = acc.shape[1]
    rows = sum(piece.shape[0] for piece in pieces)

    def kernel(place_ref, x_ref, acc_ref, *refs):
        total = acc_ref[...]
        for number, ref, first in pieces_of(refs[:-1], step):
            column = pl.multiple_of(place_ref[1 + number] * step, step)
            total = total + jnp.dot(
                x_ref[:, pl.ds(column, step)],
                ref[first : first + step, :],
                preferred_element_type=F32,
            )
        refs[-1][...] = total.astype(refs[-1].dtype)

    def whole(shape):
        return pl.BlockSpec(shape, lambda i, *_: (0, 0))

    return pl.pallas_call(
        kernel,
        grid_spec=pltpu.PrefetchScalarGridSpec(
            num_scalar_prefetch=1,
            grid=(1,),
            in_specs=[
                pl.BlockSpec((tokens, rows), lambda i, place: (0, place[0])),
                whole(acc.shape),
            ]
            + [whole(piece.shape) for piece in pieces],
            out_specs=whole(acc.shape),
        ),
        out_shape=jax.ShapeDtypeStruct(acc.shape, BF16 if last else F32),
        compiler_params=params(),
        cost_estimate=cost(2 * tokens * rows * kv, 3 << 20),
        name="more_values",
    )(place, x, acc, *pieces)


def input_grad_call(place, dv_low, rank_grad, down, pieces, step, model, so_far):
    tokens, kv = dv_low.shape
    rows = sum(piece.shape[0] for piece in pieces)
    rank = down.shape[0]
    first_call = so_far is None

    def kernel(place_ref, dv_ref, rank_ref, down_ref, *refs):
        out_ref = refs[-1]
        piece_refs = refs[: len(pieces)]
        for number, ref, first in pieces_of(piece_refs, step):
            column = pl.multiple_of(place_ref[1 + number] * step, step)
            grad = contract_trailing(dv_ref[...], ref[first : first + step, :])
            grad = grad + jnp.dot(
                rank_ref[...], down_ref[:, pl.ds(column, step)], preferred_element_type=F32
            )
            out_ref[:, pl.ds(column, step)] = grad.astype(BF16)

    def whole(shape):
        return pl.BlockSpec(shape, lambda i, *_: (0, 0))

    def shard(height):
        return pl.BlockSpec((height, rows), lambda i, place: (0, place[0]))

    operands = [place, dv_low, rank_grad, down, *pieces]
    in_specs = [whole(dv_low.shape), whole(rank_grad.shape), shard(rank)] + [
        whole(piece.shape) for piece in pieces
    ]
    aliases = {}
    if not first_call:
        aliases = {len(operands): 0}
        operands.append(so_far)
        in_specs.append(pl.BlockSpec(memory_space=pl.ANY))
    return pl.pallas_call(
        kernel,
        grid_spec=pltpu.PrefetchScalarGridSpec(
            num_scalar_prefetch=1, grid=(1,), in_specs=in_specs, out_specs=shard(tokens)
        ),
        out_shape=jax.ShapeDtypeStruct((tokens, model), BF16),
        input_output_aliases=aliases,
        compiler_params=params(),
        cost_estimate=cost(2 * tokens * rows * kv, 3 << 20),
        name="input_grad",
    )(*operands)


def adapter_grad_call(dv_own, dv_back, up, low_rank, x, parts, scale):
    tokens, model = x.shape
    rank, kv = up.shape
    width = (model + kv) // parts
    cut = 512 if model % 512 == 0 else model

    def kernel(own_ref, up_ref, low_ref, x_ref, *refs):
        back_refs = refs[: len(dv_back)]
        dv_ref, rank_ref, out_ref = refs[len(dv_back) :]
        value_grad = own_ref[...]
        for ref in back_refs:
            value_grad = value_grad + ref[...].astype(F32)
        dv_ref[...] = value_grad.astype(BF16)
        rank_grad = ADAPTER_SCALE * lax.dot_general(
            value_grad,
            up_ref[...].astype(F32),
            (((1,), (1,)), ((), ())),
            precision=lax.Precision.HIGHEST,
            preferred_element_type=F32,
        )
        rank_low = rank_grad.astype(BF16)
        rank_ref[...] = rank_low
        down = contract_leading(rank_low, x_ref[...]) * scale
        raised = contract_leading(low_ref[...], value_grad, lax.Precision.HIGHEST)
        both = jnp.concatenate([down, raised * (ADAPTER_SCALE * scale)], axis=1)
        for part in range(parts):
            out_ref[part] = both[:, part * width : (part + 1) * width]

    return pl.pallas_call(
        kernel,
        out_shape=[
            jax.ShapeDtypeStruct((tokens, kv), BF16),
            jax.ShapeDtypeStruct((tokens, rank), BF16),
            jax.ShapeDtypeStruct((parts, rank, width), F32),
        ],
        compiler_params=params(),
        cost_estimate=cost(2 * tokens * rank * model * 16, 4 << 20),
        name="adapter_grad",
    )(dv_own, up, low_rank, x, *dv_back)


def sum_everywhere(grads, here):
    seq_count = lax.axis_size("seq")
    low, high = here & 1, (here >> 1) & 1
    kept = lax.dynamic_slice_in_dim(grads, 2 * low, 2, 0)
    sent = lax.dynamic_slice_in_dim(grads, 2 - 2 * low, 2, 0)
    half = kept + flip(sent, "seq", 1)
    kept = lax.dynamic_slice_in_dim(half, high, 1, 0)
    sent = lax.dynamic_slice_in_dim(half, 1 - high, 1, 0)
    part = kept + flip(sent, "seq", 2)
    bit = 4
    while bit < seq_count:
        part = part + flip(part, "seq", bit)
        bit *= 2
    bit = 1
    while bit < lax.axis_size("fsdp"):
        part = part + flip(part, "fsdp", bit)
        bit *= 2
    other = flip(part, "seq", 2)
    half = jnp.where(
        high == 0, jnp.concatenate([part, other], 0), jnp.concatenate([other, part], 0)
    )
    other = flip(half, "seq", 1)
    return jnp.where(
        low == 0, jnp.concatenate([half, other], 0), jnp.concatenate([other, half], 0)
    )


def gather_order(seq_count):
    held = [[i] for i in range(seq_count)]
    bits = chip_bits(seq_count)
    for step in range(len(bits)):
        held = [held[i] + held[i ^ chip_mask(seq_count, step)(i)] for i in range(seq_count)]
    return np.array([held[i] + held[i ^ 1] for i in range(seq_count)], np.int32)


def chip_bits(seq_count):
    return [1 << b for b in range(1, seq_count.bit_length() - 1)]


def chip_mask(seq_count, step):
    bits = chip_bits(seq_count)
    return lambda index: bits[step] if index % 2 == 0 else bits[len(bits) - 1 - step]


def spread(part):
    seq_count = lax.axis_size("seq")
    held = [part]
    for step in range(len(chip_bits(seq_count))):
        joined = held[0] if len(held) == 1 else jnp.concatenate(held, axis=0)
        held = [joined, flip(joined, "seq", chip_mask(seq_count, step))]
    return held + [flip(block, "seq", 1) for block in held]


def body(
    normed_block_input,
    stored_rotated_queries,
    stored_rotated_keys,
    attention_output_gradient,
    frozen_value_weight,
    adapter_down_weight,
    adapter_up_weight,
    packed_document_lengths,
):
    x = normed_block_input[0]
    q = stored_rotated_queries[0]
    k = stored_rotated_keys[0]
    o = attention_output_gradient[0]
    w = frozen_value_weight
    tokens, model = x.shape
    seq_count = lax.axis_size("seq")
    fsdp_count = lax.axis_size("fsdp")
    here = lax.axis_index("seq")
    shard_number = lax.axis_index("fsdp")
    rows = w.shape[0]
    part_rows = rows // seq_count
    longest = tokens * seq_count // 4
    back = min(-(-(longest - 1) // tokens), seq_count - 1)

    own_part = lax.dynamic_slice_in_dim(w, here * part_rows, part_rows, 0)
    arrived = [turn(own_part, "fsdp", by) for by in range(1, fsdp_count)]
    key_blocks = [shift(k, "seq", by) for by in range(back, 0, -1)] + [k]

    info = jnp.concatenate([here[None], packed_document_lengths[0]]).astype(jnp.int32)
    probs, dv_blocks = probs_call(info, q, o, key_blocks)
    dv_back = [shift(dv_blocks[back - by], "seq", -by) for by in range(1, back + 1)]

    order = jnp.asarray(gather_order(seq_count))[here]
    own_place = jnp.stack([shard_number, jnp.int32(0)])
    acc, low_rank = own_values_call(own_place, x, adapter_down_weight, adapter_up_weight, w)
    dv_low, rank_grad, adapter_grads = adapter_grad_call(
        dv_blocks[back],
        dv_back,
        adapter_up_weight,
        low_rank,
        x,
        4,
        1.0 / (tokens * seq_count * fsdp_count),
    )
    input_gradient = input_grad_call(
        own_place, dv_low, rank_grad, adapter_down_weight, [w], rows, model, None
    )
    for by in range(1, fsdp_count):
        owner = (shard_number - by) % fsdp_count
        pieces = spread(arrived[by - 1])
        if part_rows % 128 == 0:
            step = part_rows
            place = jnp.concatenate([owner[None], order])
        else:
            step = rows
            joined = jnp.concatenate(pieces, axis=0).reshape(seq_count, part_rows, -1)
            pieces = [jnp.take(joined, jnp.argsort(order), axis=0).reshape(rows, -1)]
            place = jnp.stack([owner, jnp.int32(0)])
        acc = more_values_call(place, x, acc, pieces, step, by == fsdp_count - 1)
        input_gradient = input_grad_call(
            place,
            dv_low,
            rank_grad,
            adapter_down_weight,
            pieces,
            step,
            model,
            input_gradient,
        )
    value_blocks = [shift(acc, "seq", by) for by in range(back, 0, -1)] + [acc]
    rotated_query_gradient, dk_blocks = scores_grad_call(probs, q, o, key_blocks, value_blocks)
    key_gradient = dk_blocks[back]
    for by in range(1, back + 1):
        key_gradient = key_gradient + shift(dk_blocks[back - by], "seq", -by).astype(F32)

    adapter_grads = sum_everywhere(adapter_grads, here)
    adapter_grads = adapter_grads.transpose(1, 0, 2).reshape(adapter_down_weight.shape[0], -1)
    return (
        input_gradient[None],
        rotated_query_gradient[None],
        key_gradient.astype(BF16)[None],
        adapter_grads[:, :model],
        adapter_grads[:, model:],
    )


def solution(mesh):
    placed = (
        P("fsdp", "seq", None),
        P("fsdp", "seq", None),
        P("fsdp", "seq", None),
        P("fsdp", "seq", None),
        P("fsdp", None),
        P(),
        P(),
        P("fsdp", None),
    )
    return jax.shard_map(
        body,
        mesh=mesh,
        in_specs=placed,
        out_specs=(
            P("fsdp", "seq", None),
            P("fsdp", "seq", None),
            P("fsdp", "seq", None),
            P(),
            P(),
        ),
        check_vma=False,
    )
```

```python
import math

import jax
import jax.numpy as jnp
import numpy as np
from jax import lax
from jax.experimental import pallas as pl
from jax.experimental.pallas import tpu as pltpu
from jax.sharding import PartitionSpec as P

HEAD_FEATURES = 128
QUERY_HEADS = 32
KEY_VALUE_HEADS = 4
GROUP = QUERY_HEADS // KEY_VALUE_HEADS
ADAPTER_SCALE = 2.0
NEG_FILL = -1e30
INVERSE = HEAD_FEATURES ** (-0.5)
LOG2E = math.log2(math.e)
VMEM_LIMIT = 32 * 1024 * 1024
SMALL = pl.CostEstimate(flops=1, bytes_accessed=1, transcendentals=0)
F32 = jnp.float32
BF16 = jnp.bfloat16


def params():
    return pltpu.CompilerParams(vmem_limit_bytes=VMEM_LIMIT)


def contract_trailing(left, right):
    return lax.dot_general(left, right, (((1,), (1,)), ((), ())), preferred_element_type=F32)


def contract_leading(left, right, precision=None):
    return lax.dot_general(
        left, right, (((0,), (0,)), ((), ())), preferred_element_type=F32, precision=precision
    )


def flip(value, axis, mask, name="exchange"):
    size = lax.axis_size(axis)
    choose = mask if callable(mask) else (lambda index: mask)
    with jax.named_scope(name):
        return lax.ppermute(value, axis, [(i, i ^ choose(i)) for i in range(size)])


def shift(value, axis, by, name="halo"):
    size = lax.axis_size(axis)
    with jax.named_scope(name):
        return lax.ppermute(value, axis, [(i, i + by) for i in range(size) if 0 <= i + by < size])


def turn(value, axis, by, name="weight_ring"):
    size = lax.axis_size(axis)
    with jax.named_scope(name):
        return lax.ppermute(value, axis, [(i, (i + by) % size) for i in range(size)])


def after(values):
    return lax.optimization_barrier(values)


def vmem():
    return pl.BlockSpec(memory_space=pltpu.VMEM)


def smem():
    return pl.BlockSpec(memory_space=pltpu.SMEM)


def hbm():
    return pl.BlockSpec(memory_space=pltpu.HBM)


def copies(pairs, sems):
    started = []
    for number, (source, target) in enumerate(pairs):
        copy = pltpu.make_async_copy(source, target, sems.at[number])
        copy.start()
        started.append(copy)
    return started


def dma(count):
    return pltpu.SemaphoreType.DMA((count,))


def column_blocks(ref, count):
    width = ref.shape[1] // count
    return [ref.at[:, pl.ds(i * width, width)] for i in range(count)]


def head_rows(ref, head):
    first = head * GROUP
    return jnp.concatenate(
        [
            ref[:, (first + i) * HEAD_FEATURES : (first + i + 1) * HEAD_FEATURES]
            for i in range(GROUP)
        ],
        axis=0,
    )


def own_rows(tokens):
    key = lax.broadcasted_iota(jnp.int32, (tokens, GROUP * tokens), 0)
    query = lax.broadcasted_iota(jnp.int32, (tokens, GROUP * tokens), 1) % tokens
    return key <= query


def to_slots(rows, own, tokens):
    last = rows.shape[0] - tokens
    return jnp.concatenate(
        [jnp.where(own, rows[last:], rows[:tokens]), rows[tokens:last]], axis=0
    )


def from_slots(slots, own, tokens):
    shared = slots[:tokens]
    return jnp.concatenate(
        [
            jnp.where(own, 0.0, shared).astype(BF16),
            slots[tokens:].astype(BF16),
            jnp.where(own, shared, 0.0).astype(BF16),
        ],
        axis=0,
    )


HEADS_A_STEP = 2


def head_specs(tokens, slots):
    probs = pl.BlockSpec((HEADS_A_STEP, slots, GROUP * tokens), lambda step: (step, 0, 0))
    wide = pl.BlockSpec((tokens, HEADS_A_STEP * GROUP * HEAD_FEATURES), lambda step: (0, step))
    thin = pl.BlockSpec((tokens, HEADS_A_STEP * HEAD_FEATURES), lambda step: (0, step))
    return probs, wide, thin


def probs_call(me, lengths, q, o, key_blocks):
    back = len(key_blocks) - 1
    docs = lengths.shape[1]
    tokens = q.shape[0]
    kv = key_blocks[0].shape[1]
    slots = back * tokens

    def kernel(me_ref, lengths_ref, q_ref, o_ref, *refs):
        key_refs = refs[: back + 1]
        p_ref = refs[back + 1]
        dv_refs = refs[back + 2 : 2 * back + 3]
        bias_ref = refs[2 * back + 3]

        @pl.when(pl.program_id(0) == 0)
        def _():
            here = me_ref[0]
            key = lax.broadcasted_iota(jnp.int32, (slots, tokens), 0)
            query = lax.broadcasted_iota(jnp.int32, (slots, tokens), 1)
            query_place = here * tokens + query
            shared = (key < tokens) & (key <= query)
            key_place = here * tokens + jnp.where(shared, key, key - slots)
            opening = jnp.zeros((slots, tokens), jnp.int32)
            bound = jnp.int32(0)
            for doc in range(docs):
                bound = bound + lengths_ref[0, doc]
                opening = jnp.where(query_place >= bound, bound, opening)
            bias_ref[...] = jnp.where(key_place >= opening, 0.0, NEG_FILL)

        own = own_rows(tokens)
        for head in range(HEADS_A_STEP):
            columns = slice(head * HEAD_FEATURES, (head + 1) * HEAD_FEATURES)
            key_rows = jnp.concatenate([r[:, columns] for r in key_refs], axis=0)
            scores = contract_trailing(key_rows, head_rows(q_ref, head))
            scores = to_slots(scores, own, tokens)
            scores = scores + jnp.concatenate([bias_ref[...]] * GROUP, axis=1)
            peak = jnp.max(scores, axis=0, keepdims=True)
            weights = jnp.exp2((scores - peak) * (INVERSE * LOG2E))
            probs = weights * (1.0 / jnp.sum(weights, axis=0, keepdims=True))
            p_ref[head] = probs.astype(BF16)
            dv = jnp.dot(
                from_slots(probs, own, tokens),
                head_rows(o_ref, head),
                preferred_element_type=F32,
            )
            for block in range(back + 1):
                rows = dv[block * tokens : (block + 1) * tokens]
                dv_refs[block][:, columns] = rows.astype(dv_refs[block].dtype)

    probs, wide, thin = head_specs(tokens, slots)
    out = pl.pallas_call(
        kernel,
        grid=(KEY_VALUE_HEADS // HEADS_A_STEP,),
        in_specs=[smem(), smem(), wide, wide] + [thin] * (back + 1),
        out_specs=[probs] + [thin] * (back + 1),
        out_shape=[jax.ShapeDtypeStruct((KEY_VALUE_HEADS, slots, GROUP * tokens), BF16)]
        + [jax.ShapeDtypeStruct((tokens, kv), BF16)] * back
        + [jax.ShapeDtypeStruct((tokens, kv), F32)],
        scratch_shapes=[pltpu.VMEM((slots, tokens), F32)],
        compiler_params=params(),
        cost_estimate=SMALL,
        name="probs",
    )(me, lengths, q, o, *key_blocks)
    return out[0], out[1:]


def scores_grad_call(probs, q, o, key_blocks, value_blocks):
    back = len(key_blocks) - 1
    tokens = q.shape[0]
    kv = key_blocks[0].shape[1]

    def kernel(p_ref, q_ref, o_ref, *refs):
        key_refs = refs[: back + 1]
        value_refs = refs[back + 1 : 2 * back + 2]
        dq_ref = refs[2 * back + 2]
        dk_refs = refs[2 * back + 3 :]
        own = own_rows(tokens)
        for head in range(HEADS_A_STEP):
            columns = slice(head * HEAD_FEATURES, (head + 1) * HEAD_FEATURES)
            key_rows = jnp.concatenate([r[:, columns] for r in key_refs], axis=0)
            value_rows = jnp.concatenate([r[:, columns] for r in value_refs], axis=0)
            grad_probs = contract_trailing(value_rows, head_rows(o_ref, head))
            grad_probs = to_slots(grad_probs, own, tokens)
            probs = p_ref[head].astype(F32)
            mass = jnp.sum(probs, axis=0, keepdims=True)
            delta = jnp.sum(probs * grad_probs, axis=0, keepdims=True) / mass
            grad_scores = from_slots(probs * (grad_probs - delta), own, tokens)
            dk = jnp.dot(grad_scores, head_rows(q_ref, head), preferred_element_type=F32)
            dk = dk * INVERSE
            dq = jnp.dot(key_rows.T, grad_scores, preferred_element_type=F32) * INVERSE
            for i in range(GROUP):
                first = (head * GROUP + i) * HEAD_FEATURES
                dq_ref[:, first : first + HEAD_FEATURES] = (
                    dq[:, i * tokens : (i + 1) * tokens].T.astype(BF16)
                )
            for block in range(back + 1):
                rows = dk[block * tokens : (block + 1) * tokens]
                dk_refs[block][:, columns] = rows.astype(dk_refs[block].dtype)

    block, wide, thin = head_specs(tokens, probs.shape[1])
    out = pl.pallas_call(
        kernel,
        grid=(KEY_VALUE_HEADS // HEADS_A_STEP,),
        in_specs=[block, wide, wide] + [thin] * (2 * back + 2),
        out_specs=[wide] + [thin] * (back + 1),
        out_shape=[jax.ShapeDtypeStruct(q.shape, BF16)]
        + [jax.ShapeDtypeStruct((tokens, kv), BF16)] * back
        + [jax.ShapeDtypeStruct((tokens, kv), F32)],
        compiler_params=params(),
        cost_estimate=SMALL,
        name="scores_grad",
    )(probs, q, o, *key_blocks, *value_blocks)
    return out[0], out[1:]


def swap(array, name):
    return flip(array, "seq", 1, name)


def x_halves_call(me, x, shards):
    tokens, model = x.shape
    half = model // shards // 2

    def kernel(me_ref, x_hbm, mine_ref, theirs_ref, sems):
        core = me_ref[0] % 2
        pairs = []
        for which, target in ((1 - core, theirs_ref), (core, mine_ref)):
            for shard in range(shards):
                first = pl.multiple_of(2 * shard * half + which * half, half)
                pairs.append(
                    (x_hbm.at[:, pl.ds(first, half)], target.at[:, pl.ds(shard * half, half)])
                )
        for copy in copies(pairs, sems):
            copy.wait()

    return pl.pallas_call(
        kernel,
        in_specs=[smem(), hbm()],
        out_specs=[vmem()] * 2,
        out_shape=[jax.ShapeDtypeStruct((tokens, model // 2), BF16)] * 2,
        scratch_shapes=[dma(2 * shards)],
        compiler_params=params(),
        cost_estimate=SMALL,
        name="x_halves",
    )(me, x)


def put_half_call(me, out, theirs, shards):
    tokens, model = out.shape
    half = model // shards // 2

    def kernel(me_ref, theirs_ref, out_in, out_hbm, sems):
        which = 1 - me_ref[0] % 2
        pairs = []
        for shard in range(shards):
            first = pl.multiple_of(2 * shard * half + which * half, half)
            pairs.append(
                (theirs_ref.at[:, pl.ds(shard * half, half)], out_hbm.at[:, pl.ds(first, half)])
            )
        for copy in copies(pairs, sems):
            copy.wait()

    return pl.pallas_call(
        kernel,
        in_specs=[smem(), vmem(), hbm()],
        out_specs=hbm(),
        out_shape=jax.ShapeDtypeStruct((tokens, model), BF16),
        scratch_shapes=[dma(shards)],
        input_output_aliases={2: 0},
        compiler_params=params(),
        cost_estimate=SMALL,
        name="put_half",
    )(me, theirs, out)


def join_call(me, mine, theirs, shards, model):
    rank, width = mine.shape
    kv = width - model // 2
    half = model // shards // 2

    def kernel(me_ref, mine_ref, theirs_ref, down_ref, up_ref):
        core = me_ref[0] % 2
        for which, ref in ((core, mine_ref), (1 - core, theirs_ref)):
            for shard in range(shards):
                first = pl.multiple_of(2 * shard * half + which * half, half)
                down_ref[:, pl.ds(first, half)] = ref[:, shard * half : (shard + 1) * half]
        up_ref[...] = mine_ref[:, model // 2 :] + theirs_ref[:, model // 2 :]

    return pl.pallas_call(
        kernel,
        in_specs=[smem(), vmem(), vmem()],
        out_specs=[vmem()] * 2,
        out_shape=[
            jax.ShapeDtypeStruct((rank, model), F32),
            jax.ShapeDtypeStruct((rank, kv), F32),
        ],
        compiler_params=params(),
        cost_estimate=SMALL,
        name="join_adapter",
    )(me, mine, theirs)


def own_values_call(me, x_mine, x_theirs, down, up, w):
    tokens, width = x_mine.shape
    rows, kv = w.shape
    rank, model = down.shape
    half = rows // 2
    shards = model // rows

    def kernel(me_ref, mine_hbm, theirs_hbm, down_hbm, up_ref, w_hbm, acc_ref, low_ref, *scratch):
        x_ref, down_ref, w_ref, sems = scratch
        core = me_ref[0] % 2
        pairs = []
        for shard in range(shards):
            first = pl.multiple_of(shard * rows + core * half, half)
            pairs.append(
                (down_hbm.at[:, pl.ds(first, half)], down_ref.at[:, pl.ds(shard * half, half)])
            )
        pairs.append((mine_hbm, x_ref.at[pl.ds(0, tokens)]))
        pairs.append((theirs_hbm, x_ref.at[pl.ds(tokens, tokens)]))
        pairs.append((w_hbm.at[pl.ds(pl.multiple_of(core * half, half), half)], w_ref))
        for copy in copies(pairs, sems):
            copy.wait()
        low = contract_trailing(x_ref[...], down_ref[...])
        low_ref[...] = low
        adapter = jnp.dot(
            low,
            up_ref[...].astype(F32),
            precision=lax.Precision.HIGHEST,
            preferred_element_type=F32,
        )
        first = pl.multiple_of(me_ref[1] * half, half)
        acc_ref[...] = ADAPTER_SCALE * adapter + jnp.dot(
            x_ref[:, pl.ds(first, half)], w_ref[...], preferred_element_type=F32
        )

    return pl.pallas_call(
        kernel,
        in_specs=[smem(), hbm(), hbm(), hbm(), vmem(), hbm()],
        out_specs=[vmem()] * 2,
        out_shape=[
            jax.ShapeDtypeStruct((2 * tokens, kv), F32),
            jax.ShapeDtypeStruct((2 * tokens, rank), F32),
        ],
        scratch_shapes=[
            pltpu.VMEM((2 * tokens, width), BF16),
            pltpu.VMEM((rank, width), BF16),
            pltpu.VMEM((half, kv), BF16),
            dma(shards + 3),
        ],
        compiler_params=params(),
        cost_estimate=SMALL,
        name="own_values",
    )(me, x_mine, x_theirs, down, up, w)


class Pieces:
    def __init__(self, half, seq_count, fsdp_count):
        self.fsdp_count = fsdp_count
        self.half = half
        self.by_parts = (half // (seq_count // 2)) % 128 == 0
        self.step = half // (seq_count // 2) if self.by_parts else half
        self.each = half // self.step
        self.order = gather_order(seq_count)

    def chip(self, me_ref, number):
        if not self.by_parts:
            return 0
        even, odd = (int(self.order[i][number] ^ i) // 2 for i in range(2))
        here = me_ref[0]
        return lax.bitwise_xor(here // 2, jnp.where(here % 2 == 0, even, odd))

    def owner(self, me_ref, by):
        return lax.rem(me_ref[1] + (self.fsdp_count - by), self.fsdp_count)


def heights(arrays):
    firsts, first = [], 0
    for array in arrays:
        firsts.append(first)
        first += array.shape[0]
    return firsts, first


def more_values_call(me, x_mine, x_theirs, acc, shards, pieces, last):
    tokens = x_mine.shape[0]
    half, step = pieces.half, pieces.step
    bys = list(shards)
    arrays = [array for by in bys for array in shards[by]]
    firsts, rows = heights(arrays)
    count = len(bys)
    kv = acc.shape[1]

    def kernel(me_ref, acc_ref, mine_hbm, theirs_hbm, *refs):
        outs = refs[len(arrays) : -3]
        x_ref, w_ref, sems = refs[-3:]
        pairs = []
        for i, by in enumerate(bys):
            columns = pl.ds(pl.multiple_of(pieces.owner(me_ref, by) * half, half), half)
            pairs.append((mine_hbm.at[:, columns], x_ref.at[i, pl.ds(0, tokens)]))
            pairs.append((theirs_hbm.at[:, columns], x_ref.at[i, pl.ds(tokens, tokens)]))
        for ref, first, array in zip(refs, firsts, arrays):
            pairs.append((ref, w_ref.at[pl.ds(first, array.shape[0])]))
        for copy in copies(pairs, sems):
            copy.wait()
        total = acc_ref[...]
        for row in range(0, rows, step):
            i, number = row // half, (row % half) // step
            column = pl.multiple_of(pieces.chip(me_ref, number) * step, step)
            total = total + jnp.dot(
                x_ref[i, :, pl.ds(column, step)],
                w_ref[row : row + step, :],
                preferred_element_type=F32,
            )
        if last:
            outs[0][...] = total[:tokens]
            outs[1][...] = total[tokens:]
        else:
            outs[0][...] = total

    one = jax.ShapeDtypeStruct((tokens, kv), F32)
    out = pl.pallas_call(
        kernel,
        in_specs=[smem(), vmem()] + [hbm()] * (2 + len(arrays)),
        out_specs=[vmem()] * (2 if last else 1),
        out_shape=[one, one] if last else [jax.ShapeDtypeStruct(acc.shape, F32)],
        scratch_shapes=[
            pltpu.VMEM((count, 2 * tokens, half), BF16),
            pltpu.VMEM((rows, kv), BF16),
            dma(2 * count + len(arrays)),
        ],
        compiler_params=params(),
        cost_estimate=SMALL,
        name="more_values",
    )(me, acc, x_mine, x_theirs, *arrays)
    return out if last else out[0]


def input_grad_call(me, dv_mine, dv_theirs, rank_grad, down, w, shards, pieces):
    tokens, kv = dv_mine.shape
    rank, model = down.shape
    half, step = pieces.half, pieces.step
    rows = 2 * half
    bys = list(shards)
    arrays = [array for by in bys for array in shards[by]]
    firsts, _ = heights(arrays)
    count = 1 + len(bys)
    width = model // 2

    def kernel(me_ref, mine_ref, theirs_ref, rank_ref, down_hbm, w_hbm, *refs):
        out_hbm, send_hbm, down_ref, w_ref, term, buffer, sems, out_sems = refs[len(arrays) :]
        core = me_ref[0] % 2
        starts = [pl.multiple_of(i * rows + core * half, half) for i in range(count)]
        pairs = [
            (down_hbm.at[:, pl.ds(starts[i], half)], down_ref.at[:, pl.ds(i * half, half)])
            for i in range(count)
        ]
        pairs.append(
            (w_hbm.at[pl.ds(pl.multiple_of(core * half, half), half)], w_ref.at[pl.ds(0, half)])
        )
        for ref, first, array in zip(refs, firsts, arrays):
            pairs.append((ref, w_ref.at[pl.ds(half + first, array.shape[0])]))
        loads = copies(pairs, sems)
        for load in loads[: count + 1]:
            load.wait()
        term[...] = jnp.dot(rank_ref[...], down_ref[...], preferred_element_type=F32)
        dv = jnp.concatenate([mine_ref[...], theirs_ref[...]], axis=0)
        own = pl.multiple_of(me_ref[1] * half, half)
        grad = contract_trailing(dv, w_ref[0:half, :]) + term[:, pl.ds(own, half)]
        buffer[:, pl.ds(own, half)] = grad.astype(BF16)
        for load in loads[count + 1 :]:
            load.wait()
        for i, by in enumerate(bys):
            rows_of = pl.ds(half + i * half, half)
            grad = contract_trailing(dv, w_ref[rows_of, :])
            for number in range(pieces.each):
                column = pieces.owner(me_ref, by) * half + pieces.chip(me_ref, number) * step
                column = pl.multiple_of(column, step)
                part = grad[:, number * step : (number + 1) * step]
                part = part + term[:, pl.ds(column, step)]
                buffer[:, pl.ds(column, step)] = part.astype(BF16)
        pairs = [(buffer.at[pl.ds(tokens, tokens)], send_hbm)]
        for i in range(count):
            pairs.append(
                (
                    buffer.at[pl.ds(0, tokens), pl.ds(i * half, half)],
                    out_hbm.at[:, pl.ds(starts[i], half)],
                )
            )
        for copy in copies(pairs, out_sems):
            copy.wait()

    return pl.pallas_call(
        kernel,
        in_specs=[smem(), vmem(), vmem(), vmem()] + [hbm()] * (2 + len(arrays)),
        out_specs=[hbm()] * 2,
        out_shape=[
            jax.ShapeDtypeStruct((tokens, model), BF16),
            jax.ShapeDtypeStruct((tokens, width), BF16),
        ],
        scratch_shapes=[
            pltpu.VMEM((rank, width), BF16),
            pltpu.VMEM((width, kv), BF16),
            pltpu.VMEM((2 * tokens, width), F32),
            pltpu.VMEM((2 * tokens, width), BF16),
            dma(count + 1 + len(arrays)),
            dma(1 + count),
        ],
        compiler_params=params(),
        cost_estimate=SMALL,
        name="input_grad",
    )(me, dv_mine, dv_theirs, rank_grad, down, w, *arrays)


def adapter_grad_call(dv_mine, dv_theirs, up, low, x_mine, x_theirs, scale):
    tokens, width = x_mine.shape
    rank, kv = up.shape

    def kernel(mine_ref, theirs_ref, up_ref, low_ref, x_mine_hbm, x_theirs_hbm, *refs):
        rank_ref, out_ref, x_ref, sems = refs
        loads = copies(
            [
                (x_mine_hbm, x_ref.at[pl.ds(0, tokens)]),
                (x_theirs_hbm, x_ref.at[pl.ds(tokens, tokens)]),
            ],
            sems,
        )
        dv = jnp.concatenate([mine_ref[...], theirs_ref[...]], axis=0)
        rank_low = (ADAPTER_SCALE * contract_trailing(dv, up_ref[...])).astype(BF16)
        rank_ref[...] = rank_low
        raised = contract_leading(low_ref[...], dv.astype(F32), lax.Precision.HIGHEST)
        out_ref[:, width:] = raised * (ADAPTER_SCALE * scale)
        for load in loads:
            load.wait()
        out_ref[:, :width] = contract_leading(rank_low, x_ref[...]) * scale

    return pl.pallas_call(
        kernel,
        in_specs=[vmem()] * 4 + [hbm()] * 2,
        out_specs=[vmem()] * 2,
        out_shape=[
            jax.ShapeDtypeStruct((2 * tokens, rank), BF16),
            jax.ShapeDtypeStruct((rank, width + kv), F32),
        ],
        scratch_shapes=[pltpu.VMEM((2 * tokens, width), BF16), dma(2)],
        compiler_params=params(),
        cost_estimate=SMALL,
        name="adapter_grad",
    )(dv_mine, dv_theirs, up, low, x_mine, x_theirs)


def sum_steps(seq_count, fsdp_count):
    steps, bit = [], 1
    while bit < fsdp_count:
        steps.append(("fsdp", bit))
        bit *= 2
    return steps + [("seq", bit) for bit in chip_bits(seq_count)[::-1]]


def sum_step(low, step, keep=False):
    axis, mask = step
    total = low.astype(F32) + flip(low, axis, mask, "adapter_sum").astype(F32)
    return total if keep else total.astype(BF16)


def chip_bits(seq_count):
    return [1 << b for b in range(1, seq_count.bit_length() - 1)]


def chip_mask(seq_count, stage):
    bits = chip_bits(seq_count)
    return lambda index: bits[stage] if index % 2 == 0 else bits[len(bits) - 1 - stage]


def gather_order(seq_count):
    held = [[i] for i in range(seq_count)]
    for stage in range(len(chip_bits(seq_count))):
        mask = chip_mask(seq_count, stage)
        held = [held[i] + held[i ^ mask(i)] for i in range(seq_count)]
    order = np.array(held, np.int32)
    relative = order ^ np.arange(seq_count, dtype=np.int32)[:, None]
    assert (relative == relative[np.arange(seq_count) % 2]).all()
    return order


def ring_order(fsdp_count):
    return sorted(range(1, fsdp_count), key=lambda by: (min(by, fsdp_count - by), by))


def across(array, stage):
    mask = chip_mask(lax.axis_size("seq"), stage)
    return flip(array, "seq", mask, f"weight_chip_{stage}")


def spread_step(held):
    stages = len(chip_bits(lax.axis_size("seq")))
    size = len(held)
    if size == 1 << stages:
        return None
    if size == 1 and stages >= 2:
        return held + [across(held[0], 0), across(held[0], 1)]
    if size == 3:
        return held + [across(held[1], 1)]
    stage = size.bit_length() - 1
    if size == 1:
        return held + [across(held[0], stage)]
    joined = jnp.concatenate(held, axis=0)
    other = across(joined, stage)
    height = held[0].shape[0]
    return held + [other[i * height : (i + 1) * height] for i in range(size)]


def natural_half(held, order, here):
    width = held[0].shape[1]
    chips = jnp.asarray(order)[here] // 2
    joined = jnp.concatenate(held, axis=0).reshape(len(held), -1, width)
    return [jnp.take(joined, jnp.argsort(chips), axis=0).reshape(-1, width)]


def body(
    normed_block_input,
    stored_rotated_queries,
    stored_rotated_keys,
    attention_output_gradient,
    frozen_value_weight,
    adapter_down_weight,
    adapter_up_weight,
    packed_document_lengths,
):
    x = normed_block_input[0]
    q = stored_rotated_queries[0]
    k = stored_rotated_keys[0]
    o = attention_output_gradient[0]
    w = frozen_value_weight
    down, up = adapter_down_weight, adapter_up_weight
    tokens, model = x.shape
    seq_count = lax.axis_size("seq")
    fsdp_count = lax.axis_size("fsdp")
    here = lax.axis_index("seq")
    half = w.shape[0] // 2
    part_rows = half // (seq_count // 2)
    longest = tokens * seq_count // 4
    back = -(-longest // tokens)
    me = jnp.stack([here, lax.axis_index("fsdp")]).astype(jnp.int32)
    pieces = Pieces(half, seq_count, fsdp_count)
    ring = ring_order(fsdp_count)

    first_row = (here % 2) * half + (here // 2) * part_rows
    arrived = {0: lax.dynamic_slice_in_dim(w, first_row, part_rows, 0)}
    to_come = list(ring)
    held = {}

    def ring_step(count):
        for by in to_come[:count]:
            upward = 2 * by <= fsdp_count
            source = by - 1 if upward else (by + 1) % fsdp_count
            arrived[by] = turn(arrived[source], "fsdp", 1 if upward else -1)
        del to_come[:count]

    def advance(bys=ring):
        for by in list(held):
            held[by] = spread_step(held[by]) or held[by]
        for by in ring:
            if by in bys and by in ready and by not in held:
                held[by] = spread_step([arrived[by]]) or [arrived[by]]

    ready = set()

    ring_step(2)
    arrived[0], x = after((arrived[0], x))
    key_blocks = [shift(k, "seq", by, "key_halo") for by in range(back, 0, -1)] + [k]
    x_mine, x_sent = x_halves_call(me, x, fsdp_count)
    x_theirs = swap(x_sent, "x_core")
    probs, dv_blocks = probs_call(me, packed_document_lengths, q, o, key_blocks)
    arrived, dv_blocks, x_theirs = after((arrived, dv_blocks, x_theirs))
    ready.update(by for by in arrived if by)

    dv_back = [
        shift(dv_blocks[back - by], "seq", -by, "value_grad_halo") for by in range(1, back + 1)
    ]
    advance()
    ring_step(1)
    acc, low = own_values_call(me, x_mine, x_theirs, down, up, w)
    arrived, held, dv_back, acc, low = after((arrived, held, dv_back, acc, low))
    ready.update(by for by in arrived if by)

    steps = sum_steps(seq_count, fsdp_count)
    used = {}
    chips = seq_count // 2
    sums = None

    def complete():
        return {by: held[by] for by in ring if by in held and len(held[by]) == chips}

    def arrays_of(parts):
        if pieces.by_parts:
            return parts
        return {by: natural_half(parts[by], pieces.order, here) for by in parts}

    while sums is None or len(complete()) < len(ring):
        done = {by: parts for by, parts in complete().items() if by not in used}
        advance()
        ring_step(1)
        if sums is None:
            dv = dv_blocks[back]
            for block in dv_back:
                dv = dv + block.astype(F32)
            dv_mine = dv.astype(BF16)
            dv_theirs = swap(dv_mine, "value_grad_core")
            scale = 1.0 / (tokens * seq_count * fsdp_count)
            rank_grad, sums = adapter_grad_call(
                dv_mine, dv_theirs, up, low, x_mine, x_theirs, scale
            )
        if len(steps) > 2:
            sums = sum_step(sums, steps.pop(0))
        if done and len(done) == len(ring) - 1:
            acc = more_values_call(me, x_mine, x_theirs, acc, arrays_of(done), pieces, False)
            used.update(done)
        arrived, held, acc, sums = after((arrived, held, acc, sums))
        ready.update(by for by in arrived if by)
    rest = {by: held[by] for by in ring if by not in used}
    values, values_sent = more_values_call(
        me, x_mine, x_theirs, acc, arrays_of(rest), pieces, True
    )

    values = (values + swap(values_sent, "values_core")).astype(BF16)
    values, dv_mine, sums = after((values, dv_mine, sums))
    value_blocks = [shift(values, "seq", by, "value_halo") for by in range(back, 0, -1)] + [values]
    while len(steps) > 1:
        sums = sum_step(sums, steps.pop(0))
    input_grad, input_grad_sent = input_grad_call(
        me, dv_mine, dv_theirs, rank_grad, down, w, arrays_of(complete()), pieces
    )
    value_blocks, sums, input_grad_sent = after((value_blocks, sums, input_grad_sent))

    total = sum_step(sums, steps[0], keep=True) if steps else sums.astype(F32)
    rotated_query_gradient, dk_blocks = scores_grad_call(probs, q, o, key_blocks, value_blocks)
    total, input_grad_sent, dk_blocks = after((total, input_grad_sent, dk_blocks))
    dk_back = [
        shift(dk_blocks[back - by], "seq", -by, "key_grad_halo") for by in range(1, back + 1)
    ]
    total_theirs = swap(total, "adapter_core")
    input_grad_theirs = swap(input_grad_sent, "input_grad_core")
    input_gradient = put_half_call(me, input_grad, input_grad_theirs, fsdp_count)
    down_gradient, up_gradient = join_call(me, total, total_theirs, fsdp_count, model)
    dk_back, input_gradient, down_gradient, up_gradient = after(
        (dk_back, input_gradient, down_gradient, up_gradient)
    )
    key_gradient = dk_blocks[back]
    for block in dk_back:
        key_gradient = key_gradient + block.astype(F32)
    return (
        input_gradient[None],
        rotated_query_gradient[None],
        key_gradient.astype(BF16)[None],
        down_gradient,
        up_gradient,
    )


def solution(mesh):
    placed = (
        P("fsdp", "seq", None),
        P("fsdp", "seq", None),
        P("fsdp", "seq", None),
        P("fsdp", "seq", None),
        P("fsdp", None),
        P(),
        P(),
        P("fsdp", None),
    )
    return jax.shard_map(
        body,
        mesh=mesh,
        in_specs=placed,
        out_specs=(
            P("fsdp", "seq", None),
            P("fsdp", "seq", None),
            P("fsdp", "seq", None),
            P(),
            P(),
        ),
        check_vma=False,
    )
```

```python
import math

import jax
import jax.numpy as jnp
import numpy as np
from jax import lax
from jax.experimental import pallas as pl
from jax.experimental.pallas import tpu as pltpu
from jax.sharding import PartitionSpec as P

HEAD_FEATURES = 128
QUERY_HEADS = 32
KEY_VALUE_HEADS = 4
GROUP = QUERY_HEADS // KEY_VALUE_HEADS
ADAPTER_SCALE = 2.0
NEG_FILL = -1e30
INVERSE = HEAD_FEATURES ** (-0.5)
LOG2E = math.log2(math.e)
VMEM_LIMIT = 32 * 1024 * 1024
SMALL = pl.CostEstimate(flops=1, bytes_accessed=1, transcendentals=0)
F32 = jnp.float32
BF16 = jnp.bfloat16


def params():
    return pltpu.CompilerParams(vmem_limit_bytes=VMEM_LIMIT)


def contract_trailing(left, right):
    return lax.dot_general(left, right, (((1,), (1,)), ((), ())), preferred_element_type=F32)


def contract_leading(left, right, precision=None):
    return lax.dot_general(
        left, right, (((0,), (0,)), ((), ())), preferred_element_type=F32, precision=precision
    )


def flip(value, axis, mask, name="exchange"):
    size = lax.axis_size(axis)
    choose = mask if callable(mask) else (lambda index: mask)
    with jax.named_scope(name):
        return lax.ppermute(value, axis, [(i, i ^ choose(i)) for i in range(size)])


def shift(value, axis, by, name="halo"):
    size = lax.axis_size(axis)
    with jax.named_scope(name):
        return lax.ppermute(value, axis, [(i, i + by) for i in range(size) if 0 <= i + by < size])


def turn(value, axis, by, name="weight_ring"):
    size = lax.axis_size(axis)
    with jax.named_scope(name):
        return lax.ppermute(value, axis, [(i, (i + by) % size) for i in range(size)])


def after(values):
    return lax.optimization_barrier(values)


def vmem():
    return pl.BlockSpec(memory_space=pltpu.VMEM)


def smem():
    return pl.BlockSpec(memory_space=pltpu.SMEM)


def hbm():
    return pl.BlockSpec(memory_space=pltpu.HBM)


def copies(pairs, sems):
    started = []
    for number, (source, target) in enumerate(pairs):
        copy = pltpu.make_async_copy(source, target, sems.at[number])
        copy.start()
        started.append(copy)
    return started


def dma(count):
    return pltpu.SemaphoreType.DMA((count,))


def column_blocks(ref, count):
    width = ref.shape[1] // count
    return [ref.at[:, pl.ds(i * width, width)] for i in range(count)]


def head_rows(ref, head):
    first = head * GROUP
    return jnp.concatenate(
        [
            ref[:, (first + i) * HEAD_FEATURES : (first + i + 1) * HEAD_FEATURES]
            for i in range(GROUP)
        ],
        axis=0,
    )


def own_rows(tokens):
    key = lax.broadcasted_iota(jnp.int32, (tokens, GROUP * tokens), 0)
    query = lax.broadcasted_iota(jnp.int32, (tokens, GROUP * tokens), 1) % tokens
    return key <= query


def to_slots(rows, own, tokens):
    last = rows.shape[0] - tokens
    return jnp.concatenate(
        [jnp.where(own, rows[last:], rows[:tokens]), rows[tokens:last]], axis=0
    )


def from_slots(slots, own, tokens):
    shared = slots[:tokens]
    return jnp.concatenate(
        [
            jnp.where(own, 0.0, shared).astype(BF16),
            slots[tokens:].astype(BF16),
            jnp.where(own, shared, 0.0).astype(BF16),
        ],
        axis=0,
    )


HEADS_A_STEP = 2


def head_specs(tokens, slots):
    probs = pl.BlockSpec((HEADS_A_STEP, slots, GROUP * tokens), lambda step: (step, 0, 0))
    wide = pl.BlockSpec((tokens, HEADS_A_STEP * GROUP * HEAD_FEATURES), lambda step: (0, step))
    thin = pl.BlockSpec((tokens, HEADS_A_STEP * HEAD_FEATURES), lambda step: (0, step))
    return probs, wide, thin


def probs_call(me, lengths, q, o, key_blocks):
    back = len(key_blocks) - 1
    docs = lengths.shape[1]
    tokens = q.shape[0]
    kv = key_blocks[0].shape[1]
    slots = back * tokens

    def kernel(me_ref, lengths_ref, q_ref, o_ref, *refs):
        key_refs = refs[: back + 1]
        p_ref = refs[back + 1]
        dv_refs = refs[back + 2 : 2 * back + 3]
        bias_ref = refs[2 * back + 3]

        @pl.when(pl.program_id(0) == 0)
        def _():
            here = me_ref[0]
            key = lax.broadcasted_iota(jnp.int32, (slots, tokens), 0)
            query = lax.broadcasted_iota(jnp.int32, (slots, tokens), 1)
            query_place = here * tokens + query
            shared = (key < tokens) & (key <= query)
            key_place = here * tokens + jnp.where(shared, key, key - slots)
            opening = jnp.zeros((slots, tokens), jnp.int32)
            bound = jnp.int32(0)
            for doc in range(docs):
                bound = bound + lengths_ref[0, doc]
                opening = jnp.where(query_place >= bound, bound, opening)
            bias_ref[...] = jnp.where(key_place >= opening, 0.0, NEG_FILL)

        own = own_rows(tokens)
        for head in range(HEADS_A_STEP):
            columns = slice(head * HEAD_FEATURES, (head + 1) * HEAD_FEATURES)
            key_rows = jnp.concatenate([r[:, columns] for r in key_refs], axis=0)
            scores = contract_trailing(key_rows, head_rows(q_ref, head))
            scores = to_slots(scores, own, tokens)
            scores = scores + jnp.concatenate([bias_ref[...]] * GROUP, axis=1)
            peak = jnp.max(scores, axis=0, keepdims=True)
            weights = jnp.exp2((scores - peak) * (INVERSE * LOG2E))
            probs = weights * (1.0 / jnp.sum(weights, axis=0, keepdims=True))
            p_ref[head] = probs.astype(BF16)
            dv = jnp.dot(
                from_slots(probs, own, tokens),
                head_rows(o_ref, head),
                preferred_element_type=F32,
            )
            for block in range(back + 1):
                rows = dv[block * tokens : (block + 1) * tokens]
                dv_refs[block][:, columns] = rows.astype(dv_refs[block].dtype)

    probs, wide, thin = head_specs(tokens, slots)
    out = pl.pallas_call(
        kernel,
        grid=(KEY_VALUE_HEADS // HEADS_A_STEP,),
        in_specs=[smem(), smem(), wide, wide] + [thin] * (back + 1),
        out_specs=[probs] + [thin] * (back + 1),
        out_shape=[jax.ShapeDtypeStruct((KEY_VALUE_HEADS, slots, GROUP * tokens), BF16)]
        + [jax.ShapeDtypeStruct((tokens, kv), BF16)] * back
        + [jax.ShapeDtypeStruct((tokens, kv), F32)],
        scratch_shapes=[pltpu.VMEM((slots, tokens), F32)],
        compiler_params=params(),
        cost_estimate=SMALL,
        name="probs",
    )(me, lengths, q, o, *key_blocks)
    return out[0], out[1:]


def scores_grad_call(probs, q, o, key_blocks, value_blocks):
    back = len(key_blocks) - 1
    tokens = q.shape[0]
    kv = key_blocks[0].shape[1]

    def kernel(p_ref, q_ref, o_ref, *refs):
        key_refs = refs[: back + 1]
        value_refs = refs[back + 1 : 2 * back + 2]
        dq_ref = refs[2 * back + 2]
        dk_refs = refs[2 * back + 3 :]
        own = own_rows(tokens)
        for head in range(HEADS_A_STEP):
            columns = slice(head * HEAD_FEATURES, (head + 1) * HEAD_FEATURES)
            key_rows = jnp.concatenate([r[:, columns] for r in key_refs], axis=0)
            value_rows = jnp.concatenate([r[:, columns] for r in value_refs], axis=0)
            grad_probs = contract_trailing(value_rows, head_rows(o_ref, head))
            grad_probs = to_slots(grad_probs, own, tokens)
            probs = p_ref[head].astype(F32)
            mass = jnp.sum(probs, axis=0, keepdims=True)
            delta = jnp.sum(probs * grad_probs, axis=0, keepdims=True) / mass
            grad_scores = from_slots(probs * (grad_probs - delta), own, tokens)
            dk = jnp.dot(grad_scores, head_rows(q_ref, head), preferred_element_type=F32)
            dk = dk * INVERSE
            dq = jnp.dot(key_rows.T, grad_scores, preferred_element_type=F32) * INVERSE
            for i in range(GROUP):
                first = (head * GROUP + i) * HEAD_FEATURES
                dq_ref[:, first : first + HEAD_FEATURES] = (
                    dq[:, i * tokens : (i + 1) * tokens].T.astype(BF16)
                )
            for block in range(back + 1):
                rows = dk[block * tokens : (block + 1) * tokens]
                dk_refs[block][:, columns] = rows.astype(dk_refs[block].dtype)

    block, wide, thin = head_specs(tokens, probs.shape[1])
    out = pl.pallas_call(
        kernel,
        grid=(KEY_VALUE_HEADS // HEADS_A_STEP,),
        in_specs=[block, wide, wide] + [thin] * (2 * back + 2),
        out_specs=[wide] + [thin] * (back + 1),
        out_shape=[jax.ShapeDtypeStruct(q.shape, BF16)]
        + [jax.ShapeDtypeStruct((tokens, kv), BF16)] * back
        + [jax.ShapeDtypeStruct((tokens, kv), F32)],
        compiler_params=params(),
        cost_estimate=SMALL,
        name="scores_grad",
    )(probs, q, o, *key_blocks, *value_blocks)
    return out[0], out[1:]


def swap(array, name):
    return flip(array, "seq", 1, name)


def x_halves_call(me, x, shards):
    tokens, model = x.shape
    half = model // shards // 2

    def kernel(me_ref, x_hbm, mine_ref, theirs_ref, sems):
        core = me_ref[0] % 2
        pairs = []
        for which, target in ((1 - core, theirs_ref), (core, mine_ref)):
            for shard in range(shards):
                first = pl.multiple_of(2 * shard * half + which * half, half)
                pairs.append(
                    (x_hbm.at[:, pl.ds(first, half)], target.at[:, pl.ds(shard * half, half)])
                )
        for copy in copies(pairs, sems):
            copy.wait()

    return pl.pallas_call(
        kernel,
        in_specs=[smem(), hbm()],
        out_specs=[vmem()] * 2,
        out_shape=[jax.ShapeDtypeStruct((tokens, model // 2), BF16)] * 2,
        scratch_shapes=[dma(2 * shards)],
        compiler_params=params(),
        cost_estimate=SMALL,
        name="x_halves",
    )(me, x)


def put_half_call(me, out, theirs, shards):
    tokens, model = out.shape
    half = model // shards // 2

    def kernel(me_ref, theirs_ref, out_in, out_hbm, sems):
        which = 1 - me_ref[0] % 2
        pairs = []
        for shard in range(shards):
            first = pl.multiple_of(2 * shard * half + which * half, half)
            pairs.append(
                (theirs_ref.at[:, pl.ds(shard * half, half)], out_hbm.at[:, pl.ds(first, half)])
            )
        for copy in copies(pairs, sems):
            copy.wait()

    return pl.pallas_call(
        kernel,
        in_specs=[smem(), vmem(), hbm()],
        out_specs=hbm(),
        out_shape=jax.ShapeDtypeStruct((tokens, model), BF16),
        scratch_shapes=[dma(shards)],
        input_output_aliases={2: 0},
        compiler_params=params(),
        cost_estimate=SMALL,
        name="put_half",
    )(me, theirs, out)


def join_call(me, mine, theirs, shards, model):
    rank, width = mine.shape
    kv = width - model // 2
    half = model // shards // 2

    def kernel(me_ref, mine_ref, theirs_ref, down_ref, up_ref):
        core = me_ref[0] % 2
        for which, ref in ((core, mine_ref), (1 - core, theirs_ref)):
            for shard in range(shards):
                first = pl.multiple_of(2 * shard * half + which * half, half)
                down_ref[:, pl.ds(first, half)] = ref[:, shard * half : (shard + 1) * half]
        up_ref[...] = mine_ref[:, model // 2 :] + theirs_ref[:, model // 2 :]

    return pl.pallas_call(
        kernel,
        in_specs=[smem(), vmem(), vmem()],
        out_specs=[vmem()] * 2,
        out_shape=[
            jax.ShapeDtypeStruct((rank, model), F32),
            jax.ShapeDtypeStruct((rank, kv), F32),
        ],
        compiler_params=params(),
        cost_estimate=SMALL,
        name="join_adapter",
    )(me, mine, theirs)


def own_values_call(me, x_mine, x_theirs, down, up, w):
    tokens, width = x_mine.shape
    rows, kv = w.shape
    rank, model = down.shape
    half = rows // 2
    shards = model // rows

    def kernel(me_ref, mine_hbm, theirs_hbm, down_hbm, up_ref, w_hbm, acc_ref, low_ref, *scratch):
        x_ref, down_ref, w_ref, sems = scratch
        core = me_ref[0] % 2
        pairs = []
        for shard in range(shards):
            first = pl.multiple_of(shard * rows + core * half, half)
            pairs.append(
                (down_hbm.at[:, pl.ds(first, half)], down_ref.at[:, pl.ds(shard * half, half)])
            )
        pairs.append((mine_hbm, x_ref.at[pl.ds(0, tokens)]))
        pairs.append((theirs_hbm, x_ref.at[pl.ds(tokens, tokens)]))
        pairs.append((w_hbm.at[pl.ds(pl.multiple_of(core * half, half), half)], w_ref))
        for copy in copies(pairs, sems):
            copy.wait()
        low = contract_trailing(x_ref[...], down_ref[...])
        low_ref[...] = low
        adapter = jnp.dot(
            low,
            up_ref[...].astype(F32),
            precision=lax.Precision.HIGHEST,
            preferred_element_type=F32,
        )
        first = pl.multiple_of(me_ref[1] * half, half)
        acc_ref[...] = ADAPTER_SCALE * adapter + jnp.dot(
            x_ref[:, pl.ds(first, half)], w_ref[...], preferred_element_type=F32
        )

    return pl.pallas_call(
        kernel,
        in_specs=[smem(), hbm(), hbm(), hbm(), vmem(), hbm()],
        out_specs=[vmem()] * 2,
        out_shape=[
            jax.ShapeDtypeStruct((2 * tokens, kv), F32),
            jax.ShapeDtypeStruct((2 * tokens, rank), F32),
        ],
        scratch_shapes=[
            pltpu.VMEM((2 * tokens, width), BF16),
            pltpu.VMEM((rank, width), BF16),
            pltpu.VMEM((half, kv), BF16),
            dma(shards + 3),
        ],
        compiler_params=params(),
        cost_estimate=SMALL,
        name="own_values",
    )(me, x_mine, x_theirs, down, up, w)


class Pieces:
    def __init__(self, half, seq_count, fsdp_count):
        self.fsdp_count = fsdp_count
        self.half = half
        self.by_parts = (half // (seq_count // 2)) % 128 == 0
        self.step = half // (seq_count // 2) if self.by_parts else half
        self.each = half // self.step
        self.order = gather_order(seq_count)

    def chip(self, me_ref, number):
        if not self.by_parts:
            return 0
        even, odd = (int(self.order[i][number] ^ i) // 2 for i in range(2))
        here = me_ref[0]
        return lax.bitwise_xor(here // 2, jnp.where(here % 2 == 0, even, odd))

    def owner(self, me_ref, by):
        return lax.rem(me_ref[1] + (self.fsdp_count - by), self.fsdp_count)


def heights(arrays):
    firsts, first = [], 0
    for array in arrays:
        firsts.append(first)
        first += array.shape[0]
    return firsts, first


def more_values_call(me, x_mine, x_theirs, acc, shards, pieces, last):
    tokens = x_mine.shape[0]
    half, step = pieces.half, pieces.step
    bys = list(shards)
    arrays = [array for by in bys for array in shards[by]]
    firsts, rows = heights(arrays)
    count = len(bys)
    kv = acc.shape[1]

    def kernel(me_ref, acc_ref, mine_hbm, theirs_hbm, *refs):
        outs = refs[len(arrays) : -3]
        x_ref, w_ref, sems = refs[-3:]
        pairs = []
        for i, by in enumerate(bys):
            columns = pl.ds(pl.multiple_of(pieces.owner(me_ref, by) * half, half), half)
            pairs.append((mine_hbm.at[:, columns], x_ref.at[i, pl.ds(0, tokens)]))
            pairs.append((theirs_hbm.at[:, columns], x_ref.at[i, pl.ds(tokens, tokens)]))
        for ref, first, array in zip(refs, firsts, arrays):
            pairs.append((ref, w_ref.at[pl.ds(first, array.shape[0])]))
        for copy in copies(pairs, sems):
            copy.wait()
        total = acc_ref[...]
        for row in range(0, rows, step):
            i, number = row // half, (row % half) // step
            column = pl.multiple_of(pieces.chip(me_ref, number) * step, step)
            total = total + jnp.dot(
                x_ref[i, :, pl.ds(column, step)],
                w_ref[row : row + step, :],
                preferred_element_type=F32,
            )
        if last:
            outs[0][...] = total[:tokens]
            outs[1][...] = total[tokens:]
        else:
            outs[0][...] = total

    one = jax.ShapeDtypeStruct((tokens, kv), F32)
    out = pl.pallas_call(
        kernel,
        in_specs=[smem(), vmem()] + [hbm()] * (2 + len(arrays)),
        out_specs=[vmem()] * (2 if last else 1),
        out_shape=[one, one] if last else [jax.ShapeDtypeStruct(acc.shape, F32)],
        scratch_shapes=[
            pltpu.VMEM((count, 2 * tokens, half), BF16),
            pltpu.VMEM((rows, kv), BF16),
            dma(2 * count + len(arrays)),
        ],
        compiler_params=params(),
        cost_estimate=SMALL,
        name="more_values",
    )(me, acc, x_mine, x_theirs, *arrays)
    return out if last else out[0]


def input_grad_call(me, dv_mine, dv_theirs, rank_grad, down, w, shards, pieces):
    tokens, kv = dv_mine.shape
    rank, model = down.shape
    half, step = pieces.half, pieces.step
    rows = 2 * half
    bys = list(shards)
    arrays = [array for by in bys for array in shards[by]]
    firsts, _ = heights(arrays)
    count = 1 + len(bys)
    width = model // 2

    def kernel(me_ref, mine_ref, theirs_ref, rank_ref, down_hbm, w_hbm, *refs):
        out_hbm, send_hbm, down_ref, w_ref, term, buffer, sems, out_sems = refs[len(arrays) :]
        core = me_ref[0] % 2
        starts = [pl.multiple_of(i * rows + core * half, half) for i in range(count)]
        pairs = [
            (down_hbm.at[:, pl.ds(starts[i], half)], down_ref.at[:, pl.ds(i * half, half)])
            for i in range(count)
        ]
        pairs.append(
            (w_hbm.at[pl.ds(pl.multiple_of(core * half, half), half)], w_ref.at[pl.ds(0, half)])
        )
        for ref, first, array in zip(refs, firsts, arrays):
            pairs.append((ref, w_ref.at[pl.ds(half + first, array.shape[0])]))
        loads = copies(pairs, sems)
        for load in loads[: count + 1]:
            load.wait()
        term[...] = jnp.dot(rank_ref[...], down_ref[...], preferred_element_type=F32)
        dv = jnp.concatenate([mine_ref[...], theirs_ref[...]], axis=0)
        own = pl.multiple_of(me_ref[1] * half, half)
        grad = contract_trailing(dv, w_ref[0:half, :]) + term[:, pl.ds(own, half)]
        buffer[:, pl.ds(own, half)] = grad.astype(BF16)
        for load in loads[count + 1 :]:
            load.wait()
        for i, by in enumerate(bys):
            rows_of = pl.ds(half + i * half, half)
            grad = contract_trailing(dv, w_ref[rows_of, :])
            for number in range(pieces.each):
                column = pieces.owner(me_ref, by) * half + pieces.chip(me_ref, number) * step
                column = pl.multiple_of(column, step)
                part = grad[:, number * step : (number + 1) * step]
                part = part + term[:, pl.ds(column, step)]
                buffer[:, pl.ds(column, step)] = part.astype(BF16)
        pairs = [(buffer.at[pl.ds(tokens, tokens)], send_hbm)]
        for i in range(count):
            pairs.append(
                (
                    buffer.at[pl.ds(0, tokens), pl.ds(i * half, half)],
                    out_hbm.at[:, pl.ds(starts[i], half)],
                )
            )
        for copy in copies(pairs, out_sems):
            copy.wait()

    return pl.pallas_call(
        kernel,
        in_specs=[smem(), vmem(), vmem(), vmem()] + [hbm()] * (2 + len(arrays)),
        out_specs=[hbm()] * 2,
        out_shape=[
            jax.ShapeDtypeStruct((tokens, model), BF16),
            jax.ShapeDtypeStruct((tokens, width), BF16),
        ],
        scratch_shapes=[
            pltpu.VMEM((rank, width), BF16),
            pltpu.VMEM((width, kv), BF16),
            pltpu.VMEM((2 * tokens, width), F32),
            pltpu.VMEM((2 * tokens, width), BF16),
            dma(count + 1 + len(arrays)),
            dma(1 + count),
        ],
        compiler_params=params(),
        cost_estimate=SMALL,
        name="input_grad",
    )(me, dv_mine, dv_theirs, rank_grad, down, w, *arrays)


def adapter_grad_call(dv_mine, dv_theirs, up, low, x_mine, x_theirs, scale):
    tokens, width = x_mine.shape
    rank, kv = up.shape

    def kernel(mine_ref, theirs_ref, up_ref, low_ref, x_mine_hbm, x_theirs_hbm, *refs):
        rank_ref, out_ref, x_ref, sems = refs
        loads = copies(
            [
                (x_mine_hbm, x_ref.at[pl.ds(0, tokens)]),
                (x_theirs_hbm, x_ref.at[pl.ds(tokens, tokens)]),
            ],
            sems,
        )
        dv = jnp.concatenate([mine_ref[...], theirs_ref[...]], axis=0)
        rank_low = (ADAPTER_SCALE * contract_trailing(dv, up_ref[...])).astype(BF16)
        rank_ref[...] = rank_low
        raised = contract_leading(low_ref[...], dv.astype(F32), lax.Precision.HIGHEST)
        out_ref[:, width:] = raised * (ADAPTER_SCALE * scale)
        for load in loads:
            load.wait()
        out_ref[:, :width] = contract_leading(rank_low, x_ref[...]) * scale

    return pl.pallas_call(
        kernel,
        in_specs=[vmem()] * 4 + [hbm()] * 2,
        out_specs=[vmem()] * 2,
        out_shape=[
            jax.ShapeDtypeStruct((2 * tokens, rank), BF16),
            jax.ShapeDtypeStruct((rank, width + kv), F32),
        ],
        scratch_shapes=[pltpu.VMEM((2 * tokens, width), BF16), dma(2)],
        compiler_params=params(),
        cost_estimate=SMALL,
        name="adapter_grad",
    )(dv_mine, dv_theirs, up, low, x_mine, x_theirs)


def sum_steps(seq_count, fsdp_count):
    ring = [("fsdp", 1 << b) for b in range(fsdp_count.bit_length() - 1)]
    chips = [("seq", bit) for bit in chip_bits(seq_count)[::-1]]
    steps = []
    while ring or chips:
        steps += ring[:1] + chips[:1]
        ring, chips = ring[1:], chips[1:]
    return steps


def sum_step(low, step, keep=False):
    axis, mask = step
    total = low.astype(F32) + flip(low, axis, mask, "adapter_sum").astype(F32)
    return total if keep else total.astype(BF16)


def chip_bits(seq_count):
    return [1 << b for b in range(1, seq_count.bit_length() - 1)]


def chip_mask(seq_count, stage):
    bits = chip_bits(seq_count)
    return lambda index: bits[stage] if index % 2 == 0 else bits[len(bits) - 1 - stage]


def gather_order(seq_count):
    held = [[i] for i in range(seq_count)]
    for stage in range(len(chip_bits(seq_count))):
        mask = chip_mask(seq_count, stage)
        held = [held[i] + held[i ^ mask(i)] for i in range(seq_count)]
    order = np.array(held, np.int32)
    relative = order ^ np.arange(seq_count, dtype=np.int32)[:, None]
    assert (relative == relative[np.arange(seq_count) % 2]).all()
    return order


def ring_order(fsdp_count):
    return sorted(range(1, fsdp_count), key=lambda by: (min(by, fsdp_count - by), by))


def across(array, stage):
    mask = chip_mask(lax.axis_size("seq"), stage)
    return flip(array, "seq", mask, f"weight_chip_{stage}")


def spread_step(held):
    stages = len(chip_bits(lax.axis_size("seq")))
    size = len(held)
    if size == 1 << stages:
        return None
    if size == 1 and stages >= 2:
        return held + [across(held[0], 0), across(held[0], 1)]
    if size == 3:
        return held + [across(held[1], 1)]
    stage = size.bit_length() - 1
    if size == 1:
        return held + [across(held[0], stage)]
    joined = jnp.concatenate(held, axis=0)
    other = across(joined, stage)
    height = held[0].shape[0]
    return held + [other[i * height : (i + 1) * height] for i in range(size)]


def natural_half(held, order, here):
    width = held[0].shape[1]
    chips = jnp.asarray(order)[here] // 2
    joined = jnp.concatenate(held, axis=0).reshape(len(held), -1, width)
    return [jnp.take(joined, jnp.argsort(chips), axis=0).reshape(-1, width)]


def body(
    normed_block_input,
    stored_rotated_queries,
    stored_rotated_keys,
    attention_output_gradient,
    frozen_value_weight,
    adapter_down_weight,
    adapter_up_weight,
    packed_document_lengths,
):
    x = normed_block_input[0]
    q = stored_rotated_queries[0]
    k = stored_rotated_keys[0]
    o = attention_output_gradient[0]
    w = frozen_value_weight
    down, up = adapter_down_weight, adapter_up_weight
    tokens, model = x.shape
    seq_count = lax.axis_size("seq")
    fsdp_count = lax.axis_size("fsdp")
    here = lax.axis_index("seq")
    half = w.shape[0] // 2
    part_rows = half // (seq_count // 2)
    longest = tokens * seq_count // 4
    back = -(-longest // tokens)
    me = jnp.stack([here, lax.axis_index("fsdp")]).astype(jnp.int32)
    pieces = Pieces(half, seq_count, fsdp_count)
    ring = ring_order(fsdp_count)

    chips = seq_count // 2
    direct = chips == 4

    def part_of(chip):
        first_row = (here % 2) * half + chip * part_rows
        return lax.dynamic_slice_in_dim(w, first_row, part_rows, 0)

    def ring_step(known, bys, name):
        for by in bys:
            upward = 2 * by <= fsdp_count
            source = by - 1 if upward else (by + 1) % fsdp_count
            known[by] = turn(known[source], "fsdp", 1 if upward else -1, name)

    def set_out(bys):
        for by in bys:
            held[by] = spread_step([arrived[by]]) or [arrived[by]]

    held = {}
    arrived = {0: part_of(here // 2)}
    across = {0: part_of(here // 2 ^ 3)} if direct else {}

    ring_step(arrived, ring[:2], "weight_ring")
    arrived[0], x = after((arrived[0], x))
    key_blocks = [shift(k, "seq", by, "key_halo") for by in range(back, 0, -1)] + [k]
    x_mine, x_sent = x_halves_call(me, x, fsdp_count)
    x_theirs = swap(x_sent, "x_core")
    probs, dv_blocks = probs_call(me, packed_document_lengths, q, o, key_blocks)
    arrived, across, dv_blocks, x_theirs = after((arrived, across, dv_blocks, x_theirs))

    dv_back = [
        shift(dv_blocks[back - by], "seq", -by, "value_grad_halo") for by in range(1, back + 1)
    ]
    if direct:
        set_out(ring[:1])
        ring_step(across, ring[:1], "weight_ring_across")
    acc, low = own_values_call(me, x_mine, x_theirs, down, up, w)
    held, across, dv_back, acc, low = after((held, across, dv_back, acc, low))

    if direct:
        set_out(ring[1:2])
    ring_step(arrived, ring[2:], "weight_ring")
    dv = dv_blocks[back]
    for block in dv_back:
        dv = dv + block.astype(F32)
    dv_mine = dv.astype(BF16)
    dv_theirs = swap(dv_mine, "value_grad_core")
    scale = 1.0 / (tokens * seq_count * fsdp_count)
    rank_grad, sums = adapter_grad_call(dv_mine, dv_theirs, up, low, x_mine, x_theirs, scale)
    arrived, held, sums = after((arrived, held, sums))

    steps = sum_steps(seq_count, fsdp_count)
    if direct:
        set_out(ring[2:])
        ring_step(across, ring[2:], "weight_ring_across")
        held = {
            by: held[by] + [across[by]] if by in across else spread_step(held[by]) for by in ring
        }
    else:
        set_out(ring)
    if len(steps) > 3:
        sums = sum_step(sums, steps.pop(0))
    held, acc, sums = after((held, acc, sums))
    while any(len(parts) < chips for parts in held.values()):
        held = after({by: spread_step(parts) for by, parts in held.items()})

    def arrays_of(parts):
        if pieces.by_parts:
            return parts
        return {by: natural_half(parts[by], pieces.order, here) for by in parts}

    if len(steps) > 2:
        sums = sum_step(sums, steps.pop(0))
    values, values_sent = more_values_call(
        me, x_mine, x_theirs, acc, arrays_of(held), pieces, True
    )

    values = (values + swap(values_sent, "values_core")).astype(BF16)
    values, dv_mine, sums = after((values, dv_mine, sums))
    value_blocks = [shift(values, "seq", by, "value_halo") for by in range(back, 0, -1)] + [values]
    while len(steps) > 1:
        sums = sum_step(sums, steps.pop(0))
    input_grad, input_grad_sent = input_grad_call(
        me, dv_mine, dv_theirs, rank_grad, down, w, arrays_of(held), pieces
    )
    value_blocks, sums, input_grad_sent = after((value_blocks, sums, input_grad_sent))

    total = sum_step(sums, steps[0], keep=True) if steps else sums.astype(F32)
    rotated_query_gradient, dk_blocks = scores_grad_call(probs, q, o, key_blocks, value_blocks)
    total, input_grad_sent, dk_blocks = after((total, input_grad_sent, dk_blocks))
    dk_back = [
        shift(dk_blocks[back - by], "seq", -by, "key_grad_halo") for by in range(1, back + 1)
    ]
    total_theirs = swap(total, "adapter_core")
    input_grad_theirs = swap(input_grad_sent, "input_grad_core")
    input_gradient = put_half_call(me, input_grad, input_grad_theirs, fsdp_count)
    down_gradient, up_gradient = join_call(me, total, total_theirs, fsdp_count, model)
    dk_back, input_gradient, down_gradient, up_gradient = after(
        (dk_back, input_gradient, down_gradient, up_gradient)
    )
    key_gradient = dk_blocks[back]
    for block in dk_back:
        key_gradient = key_gradient + block.astype(F32)
    return (
        input_gradient[None],
        rotated_query_gradient[None],
        key_gradient.astype(BF16)[None],
        down_gradient,
        up_gradient,
    )


def solution(mesh):
    placed = (
        P("fsdp", "seq", None),
        P("fsdp", "seq", None),
        P("fsdp", "seq", None),
        P("fsdp", "seq", None),
        P("fsdp", None),
        P(),
        P(),
        P("fsdp", None),
    )
    return jax.shard_map(
        body,
        mesh=mesh,
        in_specs=placed,
        out_specs=(
            P("fsdp", "seq", None),
            P("fsdp", "seq", None),
            P("fsdp", "seq", None),
            P(),
            P(),
        ),
        check_vma=False,
    )
```

```python
import math

import jax
import jax.numpy as jnp
import numpy as np
from jax import lax
from jax.experimental import pallas as pl
from jax.experimental.pallas import tpu as pltpu
from jax.sharding import PartitionSpec as P

HEAD_FEATURES = 128
QUERY_HEADS = 32
KEY_VALUE_HEADS = 4
GROUP = QUERY_HEADS // KEY_VALUE_HEADS
ADAPTER_SCALE = 2.0
NEG_FILL = -1e30
INVERSE = HEAD_FEATURES ** (-0.5)
LOG2E = math.log2(math.e)
VMEM_LIMIT = 32 * 1024 * 1024
SMALL = pl.CostEstimate(flops=1, bytes_accessed=1, transcendentals=0)
F32 = jnp.float32
BF16 = jnp.bfloat16


def params():
    return pltpu.CompilerParams(vmem_limit_bytes=VMEM_LIMIT)


def contract_trailing(left, right):
    return lax.dot_general(left, right, (((1,), (1,)), ((), ())), preferred_element_type=F32)


def contract_leading(left, right, precision=None):
    return lax.dot_general(
        left, right, (((0,), (0,)), ((), ())), preferred_element_type=F32, precision=precision
    )


def flip(value, axis, mask, name="exchange"):
    size = lax.axis_size(axis)
    choose = mask if callable(mask) else (lambda index: mask)
    with jax.named_scope(name):
        return lax.ppermute(value, axis, [(i, i ^ choose(i)) for i in range(size)])


def shift(value, axis, by, name="halo"):
    size = lax.axis_size(axis)
    with jax.named_scope(name):
        return lax.ppermute(value, axis, [(i, i + by) for i in range(size) if 0 <= i + by < size])


def turn(value, axis, by, name="weight_ring"):
    size = lax.axis_size(axis)
    with jax.named_scope(name):
        return lax.ppermute(value, axis, [(i, (i + by) % size) for i in range(size)])


def after(values):
    return lax.optimization_barrier(values)


def vmem():
    return pl.BlockSpec(memory_space=pltpu.VMEM)


def smem():
    return pl.BlockSpec(memory_space=pltpu.SMEM)


def hbm():
    return pl.BlockSpec(memory_space=pltpu.HBM)


def copies(pairs, sems):
    started = []
    for number, (source, target) in enumerate(pairs):
        copy = pltpu.make_async_copy(source, target, sems.at[number])
        copy.start()
        started.append(copy)
    return started


def dma(count):
    return pltpu.SemaphoreType.DMA((count,))


def column_blocks(ref, count):
    width = ref.shape[1] // count
    return [ref.at[:, pl.ds(i * width, width)] for i in range(count)]


def head_rows(ref, head):
    first = head * GROUP
    return jnp.concatenate(
        [
            ref[:, (first + i) * HEAD_FEATURES : (first + i + 1) * HEAD_FEATURES]
            for i in range(GROUP)
        ],
        axis=0,
    )


def own_rows(tokens):
    key = lax.broadcasted_iota(jnp.int32, (tokens, GROUP * tokens), 0)
    query = lax.broadcasted_iota(jnp.int32, (tokens, GROUP * tokens), 1) % tokens
    return key <= query


def to_slots(rows, own, tokens):
    last = rows.shape[0] - tokens
    return jnp.concatenate(
        [jnp.where(own, rows[last:], rows[:tokens]), rows[tokens:last]], axis=0
    )


def from_slots(slots, own, tokens):
    shared = slots[:tokens]
    return jnp.concatenate(
        [
            jnp.where(own, 0.0, shared).astype(BF16),
            slots[tokens:].astype(BF16),
            jnp.where(own, shared, 0.0).astype(BF16),
        ],
        axis=0,
    )


HEADS_A_STEP = 2


def head_specs(tokens, slots):
    probs = pl.BlockSpec((HEADS_A_STEP, slots, GROUP * tokens), lambda step: (step, 0, 0))
    wide = pl.BlockSpec((tokens, HEADS_A_STEP * GROUP * HEAD_FEATURES), lambda step: (0, step))
    thin = pl.BlockSpec((tokens, HEADS_A_STEP * HEAD_FEATURES), lambda step: (0, step))
    return probs, wide, thin


def probs_call(me, lengths, q, o, key_blocks):
    back = len(key_blocks) - 1
    docs = lengths.shape[1]
    tokens = q.shape[0]
    kv = key_blocks[0].shape[1]
    slots = back * tokens

    def kernel(me_ref, lengths_ref, q_ref, o_ref, *refs):
        key_refs = refs[: back + 1]
        p_ref = refs[back + 1]
        dv_refs = refs[back + 2 : 2 * back + 3]
        bias_ref = refs[2 * back + 3]

        @pl.when(pl.program_id(0) == 0)
        def _():
            here = me_ref[0]
            key = lax.broadcasted_iota(jnp.int32, (slots, tokens), 0)
            query = lax.broadcasted_iota(jnp.int32, (slots, tokens), 1)
            query_place = here * tokens + query
            shared = (key < tokens) & (key <= query)
            key_place = here * tokens + jnp.where(shared, key, key - slots)
            opening = jnp.zeros((slots, tokens), jnp.int32)
            bound = jnp.int32(0)
            for doc in range(docs):
                bound = bound + lengths_ref[0, doc]
                opening = jnp.where(query_place >= bound, bound, opening)
            bias_ref[...] = jnp.where(key_place >= opening, 0.0, NEG_FILL)

        own = own_rows(tokens)
        for head in range(HEADS_A_STEP):
            columns = slice(head * HEAD_FEATURES, (head + 1) * HEAD_FEATURES)
            key_rows = jnp.concatenate([r[:, columns] for r in key_refs], axis=0)
            scores = contract_trailing(key_rows, head_rows(q_ref, head))
            scores = to_slots(scores, own, tokens)
            scores = scores + jnp.concatenate([bias_ref[...]] * GROUP, axis=1)
            peak = jnp.max(scores, axis=0, keepdims=True)
            weights = jnp.exp2((scores - peak) * (INVERSE * LOG2E))
            probs = weights * (1.0 / jnp.sum(weights, axis=0, keepdims=True))
            p_ref[head] = probs.astype(BF16)
            dv = jnp.dot(
                from_slots(probs, own, tokens),
                head_rows(o_ref, head),
                preferred_element_type=F32,
            )
            for block in range(back + 1):
                rows = dv[block * tokens : (block + 1) * tokens]
                dv_refs[block][:, columns] = rows.astype(dv_refs[block].dtype)

    probs, wide, thin = head_specs(tokens, slots)
    out = pl.pallas_call(
        kernel,
        grid=(KEY_VALUE_HEADS // HEADS_A_STEP,),
        in_specs=[smem(), smem(), wide, wide] + [thin] * (back + 1),
        out_specs=[probs] + [thin] * (back + 1),
        out_shape=[jax.ShapeDtypeStruct((KEY_VALUE_HEADS, slots, GROUP * tokens), BF16)]
        + [jax.ShapeDtypeStruct((tokens, kv), BF16)] * back
        + [jax.ShapeDtypeStruct((tokens, kv), F32)],
        scratch_shapes=[pltpu.VMEM((slots, tokens), F32)],
        compiler_params=params(),
        cost_estimate=SMALL,
        name="probs",
    )(me, lengths, q, o, *key_blocks)
    return out[0], out[1:]


def scores_grad_call(probs, q, o, key_blocks, value_blocks):
    back = len(key_blocks) - 1
    tokens = q.shape[0]
    kv = key_blocks[0].shape[1]

    def kernel(p_ref, q_ref, o_ref, *refs):
        key_refs = refs[: back + 1]
        value_refs = refs[back + 1 : 2 * back + 2]
        dq_ref = refs[2 * back + 2]
        dk_refs = refs[2 * back + 3 :]
        own = own_rows(tokens)
        for head in range(HEADS_A_STEP):
            columns = slice(head * HEAD_FEATURES, (head + 1) * HEAD_FEATURES)
            key_rows = jnp.concatenate([r[:, columns] for r in key_refs], axis=0)
            value_rows = jnp.concatenate([r[:, columns] for r in value_refs], axis=0)
            grad_probs = contract_trailing(value_rows, head_rows(o_ref, head))
            grad_probs = to_slots(grad_probs, own, tokens)
            probs = p_ref[head].astype(F32)
            mass = jnp.sum(probs, axis=0, keepdims=True)
            delta = jnp.sum(probs * grad_probs, axis=0, keepdims=True) / mass
            grad_scores = from_slots(probs * (grad_probs - delta), own, tokens)
            dk = jnp.dot(grad_scores, head_rows(q_ref, head), preferred_element_type=F32)
            dk = dk * INVERSE
            dq = jnp.dot(key_rows.T, grad_scores, preferred_element_type=F32) * INVERSE
            for i in range(GROUP):
                first = (head * GROUP + i) * HEAD_FEATURES
                dq_ref[:, first : first + HEAD_FEATURES] = (
                    dq[:, i * tokens : (i + 1) * tokens].T.astype(BF16)
                )
            for block in range(back + 1):
                rows = dk[block * tokens : (block + 1) * tokens]
                dk_refs[block][:, columns] = rows.astype(dk_refs[block].dtype)

    block, wide, thin = head_specs(tokens, probs.shape[1])
    out = pl.pallas_call(
        kernel,
        grid=(KEY_VALUE_HEADS // HEADS_A_STEP,),
        in_specs=[block, wide, wide] + [thin] * (2 * back + 2),
        out_specs=[wide] + [thin] * (back + 1),
        out_shape=[jax.ShapeDtypeStruct(q.shape, BF16)]
        + [jax.ShapeDtypeStruct((tokens, kv), BF16)] * back
        + [jax.ShapeDtypeStruct((tokens, kv), F32)],
        compiler_params=params(),
        cost_estimate=SMALL,
        name="scores_grad",
    )(probs, q, o, *key_blocks, *value_blocks)
    return out[0], out[1:]


def swap(array, name):
    return flip(array, "seq", 1, name)


def x_halves_call(me, x, shards):
    tokens, model = x.shape
    half = model // shards // 2

    def kernel(me_ref, x_hbm, mine_ref, theirs_ref, sems):
        core = me_ref[0] % 2
        pairs = []
        for which, target in ((1 - core, theirs_ref), (core, mine_ref)):
            for shard in range(shards):
                first = pl.multiple_of(2 * shard * half + which * half, half)
                pairs.append(
                    (x_hbm.at[:, pl.ds(first, half)], target.at[:, pl.ds(shard * half, half)])
                )
        for copy in copies(pairs, sems):
            copy.wait()

    return pl.pallas_call(
        kernel,
        in_specs=[smem(), hbm()],
        out_specs=[vmem()] * 2,
        out_shape=[jax.ShapeDtypeStruct((tokens, model // 2), BF16)] * 2,
        scratch_shapes=[dma(2 * shards)],
        compiler_params=params(),
        cost_estimate=SMALL,
        name="x_halves",
    )(me, x)


def put_half_call(me, out, theirs, shards):
    tokens, model = out.shape
    half = model // shards // 2

    def kernel(me_ref, theirs_ref, out_in, out_hbm, sems):
        which = 1 - me_ref[0] % 2
        pairs = []
        for shard in range(shards):
            first = pl.multiple_of(2 * shard * half + which * half, half)
            pairs.append(
                (theirs_ref.at[:, pl.ds(shard * half, half)], out_hbm.at[:, pl.ds(first, half)])
            )
        for copy in copies(pairs, sems):
            copy.wait()

    return pl.pallas_call(
        kernel,
        in_specs=[smem(), vmem(), hbm()],
        out_specs=hbm(),
        out_shape=jax.ShapeDtypeStruct((tokens, model), BF16),
        scratch_shapes=[dma(shards)],
        input_output_aliases={2: 0},
        compiler_params=params(),
        cost_estimate=SMALL,
        name="put_half",
    )(me, theirs, out)


def join_call(me, mine, theirs, shards, model):
    rank, width = mine.shape
    kv = width - model // 2
    half = model // shards // 2

    def kernel(me_ref, mine_ref, theirs_ref, down_ref, up_ref):
        core = me_ref[0] % 2
        for which, ref in ((core, mine_ref), (1 - core, theirs_ref)):
            for shard in range(shards):
                first = pl.multiple_of(2 * shard * half + which * half, half)
                down_ref[:, pl.ds(first, half)] = ref[:, shard * half : (shard + 1) * half]
        up_ref[...] = mine_ref[:, model // 2 :] + theirs_ref[:, model // 2 :]

    return pl.pallas_call(
        kernel,
        in_specs=[smem(), vmem(), vmem()],
        out_specs=[vmem()] * 2,
        out_shape=[
            jax.ShapeDtypeStruct((rank, model), F32),
            jax.ShapeDtypeStruct((rank, kv), F32),
        ],
        compiler_params=params(),
        cost_estimate=SMALL,
        name="join_adapter",
    )(me, mine, theirs)


def own_values_call(me, x_mine, x_theirs, down, up, w):
    tokens, width = x_mine.shape
    rows, kv = w.shape
    rank, model = down.shape
    half = rows // 2
    shards = model // rows

    def kernel(me_ref, mine_hbm, theirs_hbm, down_hbm, up_ref, w_hbm, acc_ref, low_ref, *scratch):
        x_ref, down_ref, w_ref, sems = scratch
        core = me_ref[0] % 2
        pairs = []
        for shard in range(shards):
            first = pl.multiple_of(shard * rows + core * half, half)
            pairs.append(
                (down_hbm.at[:, pl.ds(first, half)], down_ref.at[:, pl.ds(shard * half, half)])
            )
        pairs.append((mine_hbm, x_ref.at[pl.ds(0, tokens)]))
        pairs.append((theirs_hbm, x_ref.at[pl.ds(tokens, tokens)]))
        pairs.append((w_hbm.at[pl.ds(pl.multiple_of(core * half, half), half)], w_ref))
        for copy in copies(pairs, sems):
            copy.wait()
        low = contract_trailing(x_ref[...], down_ref[...])
        low_ref[...] = low
        adapter = jnp.dot(
            low,
            up_ref[...].astype(F32),
            precision=lax.Precision.HIGHEST,
            preferred_element_type=F32,
        )
        first = pl.multiple_of(me_ref[1] * half, half)
        acc_ref[...] = ADAPTER_SCALE * adapter + jnp.dot(
            x_ref[:, pl.ds(first, half)], w_ref[...], preferred_element_type=F32
        )

    return pl.pallas_call(
        kernel,
        in_specs=[smem(), hbm(), hbm(), hbm(), vmem(), hbm()],
        out_specs=[vmem()] * 2,
        out_shape=[
            jax.ShapeDtypeStruct((2 * tokens, kv), F32),
            jax.ShapeDtypeStruct((2 * tokens, rank), F32),
        ],
        scratch_shapes=[
            pltpu.VMEM((2 * tokens, width), BF16),
            pltpu.VMEM((rank, width), BF16),
            pltpu.VMEM((half, kv), BF16),
            dma(shards + 3),
        ],
        compiler_params=params(),
        cost_estimate=SMALL,
        name="own_values",
    )(me, x_mine, x_theirs, down, up, w)


class Pieces:
    def __init__(self, half, seq_count, fsdp_count):
        self.fsdp_count = fsdp_count
        self.half = half
        self.by_parts = (half // (seq_count // 2)) % 128 == 0
        self.step = half // (seq_count // 2) if self.by_parts else half
        self.each = half // self.step
        self.order = gather_order(seq_count)

    def chip(self, me_ref, number):
        if not self.by_parts:
            return 0
        even, odd = (int(self.order[i][number] ^ i) // 2 for i in range(2))
        here = me_ref[0]
        return lax.bitwise_xor(here // 2, jnp.where(here % 2 == 0, even, odd))

    def owner(self, me_ref, by):
        return lax.rem(me_ref[1] + (self.fsdp_count - by), self.fsdp_count)


def heights(arrays):
    firsts, first = [], 0
    for array in arrays:
        firsts.append(first)
        first += array.shape[0]
    return firsts, first


def more_values_call(me, x_mine, x_theirs, acc, shards, pieces, last):
    tokens = x_mine.shape[0]
    half, step = pieces.half, pieces.step
    bys = list(shards)
    arrays = [array for by in bys for array in shards[by]]
    firsts, rows = heights(arrays)
    count = len(bys)
    kv = acc.shape[1]

    def kernel(me_ref, acc_ref, mine_hbm, theirs_hbm, *refs):
        outs = refs[len(arrays) : -3]
        x_ref, w_ref, sems = refs[-3:]
        pairs = []
        for i, by in enumerate(bys):
            columns = pl.ds(pl.multiple_of(pieces.owner(me_ref, by) * half, half), half)
            pairs.append((mine_hbm.at[:, columns], x_ref.at[i, pl.ds(0, tokens)]))
            pairs.append((theirs_hbm.at[:, columns], x_ref.at[i, pl.ds(tokens, tokens)]))
        for ref, first, array in zip(refs, firsts, arrays):
            pairs.append((ref, w_ref.at[pl.ds(first, array.shape[0])]))
        for copy in copies(pairs, sems):
            copy.wait()
        total = acc_ref[...]
        for row in range(0, rows, step):
            i, number = row // half, (row % half) // step
            column = pl.multiple_of(pieces.chip(me_ref, number) * step, step)
            total = total + jnp.dot(
                x_ref[i, :, pl.ds(column, step)],
                w_ref[row : row + step, :],
                preferred_element_type=F32,
            )
        if last:
            outs[0][...] = total[:tokens]
            outs[1][...] = total[tokens:]
        else:
            outs[0][...] = total

    one = jax.ShapeDtypeStruct((tokens, kv), F32)
    out = pl.pallas_call(
        kernel,
        in_specs=[smem(), vmem()] + [hbm()] * (2 + len(arrays)),
        out_specs=[vmem()] * (2 if last else 1),
        out_shape=[one, one] if last else [jax.ShapeDtypeStruct(acc.shape, F32)],
        scratch_shapes=[
            pltpu.VMEM((count, 2 * tokens, half), BF16),
            pltpu.VMEM((rows, kv), BF16),
            dma(2 * count + len(arrays)),
        ],
        compiler_params=params(),
        cost_estimate=SMALL,
        name="more_values",
    )(me, acc, x_mine, x_theirs, *arrays)
    return out if last else out[0]


def input_grad_call(me, dv_mine, dv_theirs, rank_grad, down, w, shards, pieces):
    tokens, kv = dv_mine.shape
    rank, model = down.shape
    half, step = pieces.half, pieces.step
    rows = 2 * half
    bys = list(shards)
    arrays = [array for by in bys for array in shards[by]]
    firsts, _ = heights(arrays)
    count = 1 + len(bys)
    width = model // 2

    def kernel(me_ref, mine_ref, theirs_ref, rank_ref, down_hbm, w_hbm, *refs):
        out_hbm, send_hbm, down_ref, w_ref, term, buffer, sems, out_sems = refs[len(arrays) :]
        core = me_ref[0] % 2
        starts = [pl.multiple_of(i * rows + core * half, half) for i in range(count)]
        pairs = [
            (down_hbm.at[:, pl.ds(starts[i], half)], down_ref.at[:, pl.ds(i * half, half)])
            for i in range(count)
        ]
        pairs.append(
            (w_hbm.at[pl.ds(pl.multiple_of(core * half, half), half)], w_ref.at[pl.ds(0, half)])
        )
        for ref, first, array in zip(refs, firsts, arrays):
            pairs.append((ref, w_ref.at[pl.ds(half + first, array.shape[0])]))
        loads = copies(pairs, sems)
        for load in loads[: count + 1]:
            load.wait()
        term[...] = jnp.dot(rank_ref[...], down_ref[...], preferred_element_type=F32)
        dv = jnp.concatenate([mine_ref[...], theirs_ref[...]], axis=0)
        own = pl.multiple_of(me_ref[1] * half, half)
        grad = contract_trailing(dv, w_ref[0:half, :]) + term[:, pl.ds(own, half)]
        buffer[:, pl.ds(own, half)] = grad.astype(BF16)
        for load in loads[count + 1 :]:
            load.wait()
        for i, by in enumerate(bys):
            rows_of = pl.ds(half + i * half, half)
            grad = contract_trailing(dv, w_ref[rows_of, :])
            for number in range(pieces.each):
                column = pieces.owner(me_ref, by) * half + pieces.chip(me_ref, number) * step
                column = pl.multiple_of(column, step)
                part = grad[:, number * step : (number + 1) * step]
                part = part + term[:, pl.ds(column, step)]
                buffer[:, pl.ds(column, step)] = part.astype(BF16)
        pairs = [(buffer.at[pl.ds(tokens, tokens)], send_hbm)]
        for i in range(count):
            pairs.append(
                (
                    buffer.at[pl.ds(0, tokens), pl.ds(i * half, half)],
                    out_hbm.at[:, pl.ds(starts[i], half)],
                )
            )
        for copy in copies(pairs, out_sems):
            copy.wait()

    return pl.pallas_call(
        kernel,
        in_specs=[smem(), vmem(), vmem(), vmem()] + [hbm()] * (2 + len(arrays)),
        out_specs=[hbm()] * 2,
        out_shape=[
            jax.ShapeDtypeStruct((tokens, model), BF16),
            jax.ShapeDtypeStruct((tokens, width), BF16),
        ],
        scratch_shapes=[
            pltpu.VMEM((rank, width), BF16),
            pltpu.VMEM((width, kv), BF16),
            pltpu.VMEM((2 * tokens, width), F32),
            pltpu.VMEM((2 * tokens, width), BF16),
            dma(count + 1 + len(arrays)),
            dma(1 + count),
        ],
        compiler_params=params(),
        cost_estimate=SMALL,
        name="input_grad",
    )(me, dv_mine, dv_theirs, rank_grad, down, w, *arrays)


def adapter_grad_call(dv_mine, dv_theirs, up, low, x_mine, x_theirs, scale):
    tokens, width = x_mine.shape
    rank, kv = up.shape

    def kernel(mine_ref, theirs_ref, up_ref, low_ref, x_mine_hbm, x_theirs_hbm, *refs):
        rank_ref, out_ref, x_ref, sems = refs
        loads = copies(
            [
                (x_mine_hbm, x_ref.at[pl.ds(0, tokens)]),
                (x_theirs_hbm, x_ref.at[pl.ds(tokens, tokens)]),
            ],
            sems,
        )
        dv = jnp.concatenate([mine_ref[...], theirs_ref[...]], axis=0)
        rank_low = (ADAPTER_SCALE * contract_trailing(dv, up_ref[...])).astype(BF16)
        rank_ref[...] = rank_low
        raised = contract_leading(low_ref[...], dv.astype(F32), lax.Precision.HIGHEST)
        out_ref[:, width:] = raised * (ADAPTER_SCALE * scale)
        for load in loads:
            load.wait()
        out_ref[:, :width] = contract_leading(rank_low, x_ref[...]) * scale

    return pl.pallas_call(
        kernel,
        in_specs=[vmem()] * 4 + [hbm()] * 2,
        out_specs=[vmem()] * 2,
        out_shape=[
            jax.ShapeDtypeStruct((2 * tokens, rank), BF16),
            jax.ShapeDtypeStruct((rank, width + kv), F32),
        ],
        scratch_shapes=[pltpu.VMEM((2 * tokens, width), BF16), dma(2)],
        compiler_params=params(),
        cost_estimate=SMALL,
        name="adapter_grad",
    )(dv_mine, dv_theirs, up, low, x_mine, x_theirs)


def sum_steps(seq_count, fsdp_count):
    ring = [("fsdp", 1 << b) for b in range(fsdp_count.bit_length() - 1)]
    chips = [("seq", bit) for bit in chip_bits(seq_count)[::-1]]
    steps = []
    while ring or chips:
        steps += ring[:1] + chips[:1]
        ring, chips = ring[1:], chips[1:]
    return steps


def sum_step(low, step, keep=False):
    axis, mask = step
    total = low.astype(F32) + flip(low, axis, mask, "adapter_sum").astype(F32)
    return total if keep else total.astype(BF16)


def chip_bits(seq_count):
    return [1 << b for b in range(1, seq_count.bit_length() - 1)]


def chip_mask(seq_count, stage):
    bits = chip_bits(seq_count)
    return lambda index: bits[stage] if index % 2 == 0 else bits[len(bits) - 1 - stage]


def gather_order(seq_count):
    held = [[i] for i in range(seq_count)]
    for stage in range(len(chip_bits(seq_count))):
        mask = chip_mask(seq_count, stage)
        held = [held[i] + held[i ^ mask(i)] for i in range(seq_count)]
    order = np.array(held, np.int32)
    relative = order ^ np.arange(seq_count, dtype=np.int32)[:, None]
    assert (relative == relative[np.arange(seq_count) % 2]).all()
    return order


def ring_order(fsdp_count):
    return sorted(range(1, fsdp_count), key=lambda by: (min(by, fsdp_count - by), by))


def across(array, stage):
    mask = chip_mask(lax.axis_size("seq"), stage)
    return flip(array, "seq", mask, f"weight_chip_{stage}")


def spread_step(held):
    stages = len(chip_bits(lax.axis_size("seq")))
    size = len(held)
    if size == 1 << stages:
        return None
    if size == 1 and stages >= 2:
        return held + [across(held[0], 0), across(held[0], 1)]
    if size == 3:
        return held + [across(held[1], 1)]
    stage = size.bit_length() - 1
    if size == 1:
        return held + [across(held[0], stage)]
    joined = jnp.concatenate(held, axis=0)
    other = across(joined, stage)
    height = held[0].shape[0]
    return held + [other[i * height : (i + 1) * height] for i in range(size)]


def natural_half(held, order, here):
    width = held[0].shape[1]
    chips = jnp.asarray(order)[here] // 2
    joined = jnp.concatenate(held, axis=0).reshape(len(held), -1, width)
    return [jnp.take(joined, jnp.argsort(chips), axis=0).reshape(-1, width)]


def body(
    normed_block_input,
    stored_rotated_queries,
    stored_rotated_keys,
    attention_output_gradient,
    frozen_value_weight,
    adapter_down_weight,
    adapter_up_weight,
    packed_document_lengths,
):
    x = normed_block_input[0]
    q = stored_rotated_queries[0]
    k = stored_rotated_keys[0]
    o = attention_output_gradient[0]
    w = frozen_value_weight
    down, up = adapter_down_weight, adapter_up_weight
    tokens, model = x.shape
    seq_count = lax.axis_size("seq")
    fsdp_count = lax.axis_size("fsdp")
    here = lax.axis_index("seq")
    half = w.shape[0] // 2
    part_rows = half // (seq_count // 2)
    longest = tokens * seq_count // 4
    back = -(-longest // tokens)
    me = jnp.stack([here, lax.axis_index("fsdp")]).astype(jnp.int32)
    pieces = Pieces(half, seq_count, fsdp_count)
    ring = ring_order(fsdp_count)

    chips = seq_count // 2
    direct = chips == 4

    def part_of(chip):
        first_row = (here % 2) * half + chip * part_rows
        return lax.dynamic_slice_in_dim(w, first_row, part_rows, 0)

    def ring_step(known, bys, name):
        for by in bys:
            upward = 2 * by <= fsdp_count
            source = by - 1 if upward else (by + 1) % fsdp_count
            known[by] = turn(known[source], "fsdp", 1 if upward else -1, name)

    def set_out(bys):
        for by in bys:
            held[by] = spread_step([arrived[by]]) or [arrived[by]]

    held = {}
    arrived = {0: part_of(here // 2)}
    across = {0: part_of(here // 2 ^ 3)} if direct else {}

    ring_step(arrived, ring[:2], "weight_ring")
    arrived[0], x = after((arrived[0], x))
    key_blocks = [shift(k, "seq", by, "key_halo") for by in range(back, 0, -1)] + [k]
    x_mine, x_sent = x_halves_call(me, x, fsdp_count)
    probs, dv_blocks = probs_call(me, packed_document_lengths, q, o, key_blocks)
    arrived, across, dv_blocks, x_mine, x_sent = after(
        (arrived, across, dv_blocks, x_mine, x_sent)
    )

    dv_back = [
        shift(dv_blocks[back - by], "seq", -by, "value_grad_halo") for by in range(1, back + 1)
    ]
    ring_step(arrived, ring[2:], "weight_ring")
    if direct:
        set_out(ring[:1])
    x_theirs = swap(x_sent, "x_core")
    acc, low = own_values_call(me, x_mine, x_theirs, down, up, w)
    held, arrived, dv_back, acc, low = after((held, arrived, dv_back, acc, low))

    if direct:
        set_out(ring[1:2])
        ring_step(across, ring[:1], "weight_ring_across")
    dv = dv_blocks[back]
    for block in dv_back:
        dv = dv + block.astype(F32)
    dv_mine = dv.astype(BF16)
    dv_theirs = swap(dv_mine, "value_grad_core")
    scale = 1.0 / (tokens * seq_count * fsdp_count)
    rank_grad, sums = adapter_grad_call(dv_mine, dv_theirs, up, low, x_mine, x_theirs, scale)
    across, held, sums = after((across, held, sums))

    steps = sum_steps(seq_count, fsdp_count)
    if direct:
        set_out(ring[2:])
        ring_step(across, ring[2:], "weight_ring_across")
        held = {
            by: held[by] + [across[by]] if by in across else spread_step(held[by]) for by in ring
        }
    else:
        set_out(ring)
    if len(steps) > 3:
        sums = sum_step(sums, steps.pop(0))
    held, acc, sums = after((held, acc, sums))
    while any(len(parts) < chips for parts in held.values()):
        held = after({by: spread_step(parts) for by, parts in held.items()})

    def arrays_of(parts):
        if pieces.by_parts:
            return parts
        return {by: natural_half(parts[by], pieces.order, here) for by in parts}

    if len(steps) > 2:
        sums = sum_step(sums, steps.pop(0))
    values, values_sent = more_values_call(
        me, x_mine, x_theirs, acc, arrays_of(held), pieces, True
    )

    values = (values + swap(values_sent, "values_core")).astype(BF16)
    values, dv_mine, sums = after((values, dv_mine, sums))
    value_blocks = [shift(values, "seq", by, "value_halo") for by in range(back, 0, -1)] + [values]
    while len(steps) > 1:
        sums = sum_step(sums, steps.pop(0))
    input_grad, input_grad_sent = input_grad_call(
        me, dv_mine, dv_theirs, rank_grad, down, w, arrays_of(held), pieces
    )
    value_blocks, sums, input_grad_sent = after((value_blocks, sums, input_grad_sent))

    total = sum_step(sums, steps[0], keep=True) if steps else sums.astype(F32)
    rotated_query_gradient, dk_blocks = scores_grad_call(probs, q, o, key_blocks, value_blocks)
    total, input_grad_sent, dk_blocks = after((total, input_grad_sent, dk_blocks))
    dk_back = [
        shift(dk_blocks[back - by], "seq", -by, "key_grad_halo") for by in range(1, back + 1)
    ]
    total_theirs = swap(total, "adapter_core")
    input_grad_theirs = swap(input_grad_sent, "input_grad_core")
    input_gradient = put_half_call(me, input_grad, input_grad_theirs, fsdp_count)
    down_gradient, up_gradient = join_call(me, total, total_theirs, fsdp_count, model)
    dk_back, input_gradient, down_gradient, up_gradient = after(
        (dk_back, input_gradient, down_gradient, up_gradient)
    )
    key_gradient = dk_blocks[back]
    for block in dk_back:
        key_gradient = key_gradient + block.astype(F32)
    return (
        input_gradient[None],
        rotated_query_gradient[None],
        key_gradient.astype(BF16)[None],
        down_gradient,
        up_gradient,
    )


def solution(mesh):
    placed = (
        P("fsdp", "seq", None),
        P("fsdp", "seq", None),
        P("fsdp", "seq", None),
        P("fsdp", "seq", None),
        P("fsdp", None),
        P(),
        P(),
        P("fsdp", None),
    )
    return jax.shard_map(
        body,
        mesh=mesh,
        in_specs=placed,
        out_specs=(
            P("fsdp", "seq", None),
            P("fsdp", "seq", None),
            P("fsdp", "seq", None),
            P(),
            P(),
        ),
        check_vma=False,
    )
```

```python
import math

import jax
import jax.numpy as jnp
import numpy as np
from jax import lax
from jax.experimental import pallas as pl
from jax.experimental.pallas import tpu as pltpu
from jax.sharding import PartitionSpec as P

HEAD_FEATURES = 128
QUERY_HEADS = 32
KEY_VALUE_HEADS = 4
GROUP = QUERY_HEADS // KEY_VALUE_HEADS
ADAPTER_SCALE = 2.0
NEG_FILL = -1e30
INVERSE = HEAD_FEATURES ** (-0.5)
LOG2E = math.log2(math.e)
VMEM_LIMIT = 32 * 1024 * 1024
SMALL = pl.CostEstimate(flops=1, bytes_accessed=1, transcendentals=0)
F32 = jnp.float32
BF16 = jnp.bfloat16


def params():
    return pltpu.CompilerParams(vmem_limit_bytes=VMEM_LIMIT)


def contract_trailing(left, right):
    return lax.dot_general(left, right, (((1,), (1,)), ((), ())), preferred_element_type=F32)


def contract_leading(left, right, precision=None):
    return lax.dot_general(
        left, right, (((0,), (0,)), ((), ())), preferred_element_type=F32, precision=precision
    )


def flip(value, axis, mask, name="exchange"):
    size = lax.axis_size(axis)
    choose = mask if callable(mask) else (lambda index: mask)
    with jax.named_scope(name):
        return lax.ppermute(value, axis, [(i, i ^ choose(i)) for i in range(size)])


def shift(value, axis, by, name="halo"):
    size = lax.axis_size(axis)
    with jax.named_scope(name):
        return lax.ppermute(value, axis, [(i, i + by) for i in range(size) if 0 <= i + by < size])


def turn(value, axis, by, name="weight_ring"):
    size = lax.axis_size(axis)
    with jax.named_scope(name):
        return lax.ppermute(value, axis, [(i, (i + by) % size) for i in range(size)])


def after(values):
    return lax.optimization_barrier(values)


def vmem():
    return pl.BlockSpec(memory_space=pltpu.VMEM)


def smem():
    return pl.BlockSpec(memory_space=pltpu.SMEM)


def hbm():
    return pl.BlockSpec(memory_space=pltpu.HBM)


def copies(pairs, sems):
    started = []
    for number, (source, target) in enumerate(pairs):
        copy = pltpu.make_async_copy(source, target, sems.at[number])
        copy.start()
        started.append(copy)
    return started


def dma(count):
    return pltpu.SemaphoreType.DMA((count,))


def column_blocks(ref, count):
    width = ref.shape[1] // count
    return [ref.at[:, pl.ds(i * width, width)] for i in range(count)]


def head_rows(ref, head):
    first = head * GROUP
    return jnp.concatenate(
        [
            ref[:, (first + i) * HEAD_FEATURES : (first + i + 1) * HEAD_FEATURES]
            for i in range(GROUP)
        ],
        axis=0,
    )


def own_rows(tokens):
    key = lax.broadcasted_iota(jnp.int32, (tokens, GROUP * tokens), 0)
    query = lax.broadcasted_iota(jnp.int32, (tokens, GROUP * tokens), 1) % tokens
    return key <= query


def to_slots(rows, own, tokens):
    last = rows.shape[0] - tokens
    return jnp.concatenate(
        [jnp.where(own, rows[last:], rows[:tokens]), rows[tokens:last]], axis=0
    )


def from_slots(slots, own, tokens):
    shared = slots[:tokens]
    return jnp.concatenate(
        [
            jnp.where(own, 0.0, shared).astype(BF16),
            slots[tokens:].astype(BF16),
            jnp.where(own, shared, 0.0).astype(BF16),
        ],
        axis=0,
    )


def probs_call(me, q, o, key_blocks):
    back = len(key_blocks) - 1
    docs = me.shape[0] - 2
    tokens = q.shape[0]
    kv = key_blocks[0].shape[1]
    slots = back * tokens

    def kernel(me_ref, q_ref, o_ref, *refs):
        key_refs = refs[: back + 1]
        p_ref = refs[back + 1]
        dv_refs = refs[back + 2 : 2 * back + 3]
        bias_ref = refs[2 * back + 3]

        def fill_bias():
            here = me_ref[0]
            key = lax.broadcasted_iota(jnp.int32, (slots, tokens), 0)
            query = lax.broadcasted_iota(jnp.int32, (slots, tokens), 1)
            query_place = here * tokens + query
            shared = (key < tokens) & (key <= query)
            key_place = here * tokens + jnp.where(shared, key, key - slots)
            opening = jnp.zeros((slots, tokens), jnp.int32)
            bound = jnp.int32(0)
            for doc in range(docs):
                bound = bound + me_ref[2 + doc]
                opening = jnp.where(query_place >= bound, bound, opening)
            bias_ref[...] = jnp.where(key_place >= opening, 0.0, NEG_FILL)

        fill_bias()
        own = own_rows(tokens)
        for head in range(KEY_VALUE_HEADS):
            columns = slice(head * HEAD_FEATURES, (head + 1) * HEAD_FEATURES)
            key_rows = jnp.concatenate([r[:, columns] for r in key_refs], axis=0)
            scores = contract_trailing(key_rows, head_rows(q_ref, head))
            scores = to_slots(scores, own, tokens)
            scores = scores + jnp.concatenate([bias_ref[...]] * GROUP, axis=1)
            peak = jnp.max(scores, axis=0, keepdims=True)
            weights = jnp.exp2((scores - peak) * (INVERSE * LOG2E))
            probs = weights * (1.0 / jnp.sum(weights, axis=0, keepdims=True))
            p_ref[head] = probs.astype(BF16)
            dv = jnp.dot(
                from_slots(probs, own, tokens),
                head_rows(o_ref, head),
                preferred_element_type=F32,
            )
            for block in range(back + 1):
                rows = dv[block * tokens : (block + 1) * tokens]
                dv_refs[block][:, columns] = rows.astype(dv_refs[block].dtype)

    out = pl.pallas_call(
        kernel,
        in_specs=[smem()] + [vmem()] * (back + 3),
        out_specs=[vmem()] * (back + 2),
        out_shape=[jax.ShapeDtypeStruct((KEY_VALUE_HEADS, slots, GROUP * tokens), BF16)]
        + [jax.ShapeDtypeStruct((tokens, kv), BF16)] * back
        + [jax.ShapeDtypeStruct((tokens, kv), F32)],
        scratch_shapes=[pltpu.VMEM((slots, tokens), F32)],
        compiler_params=params(),
        cost_estimate=SMALL,
        name="probs",
    )(me, q, o, *key_blocks)
    return out[0], out[1:]


def scores_grad_call(probs, q, o, key_blocks, value_blocks):
    back = len(key_blocks) - 1
    tokens = q.shape[0]
    kv = key_blocks[0].shape[1]

    def kernel(p_ref, q_ref, o_ref, *refs):
        key_refs = refs[: back + 1]
        value_refs = refs[back + 1 : 2 * back + 2]
        dq_ref = refs[2 * back + 2]
        dk_refs = refs[2 * back + 3 :]
        own = own_rows(tokens)
        for head in range(KEY_VALUE_HEADS):
            columns = slice(head * HEAD_FEATURES, (head + 1) * HEAD_FEATURES)
            key_rows = jnp.concatenate([r[:, columns] for r in key_refs], axis=0)
            value_rows = jnp.concatenate([r[:, columns] for r in value_refs], axis=0)
            grad_probs = contract_trailing(value_rows, head_rows(o_ref, head))
            grad_probs = to_slots(grad_probs, own, tokens)
            probs = p_ref[head].astype(F32)
            mass = jnp.sum(probs, axis=0, keepdims=True)
            delta = jnp.sum(probs * grad_probs, axis=0, keepdims=True) / mass
            grad_scores = from_slots(probs * (grad_probs - delta), own, tokens)
            dk = jnp.dot(grad_scores, head_rows(q_ref, head), preferred_element_type=F32)
            dk = dk * INVERSE
            dq = jnp.dot(key_rows.T, grad_scores, preferred_element_type=F32) * INVERSE
            for i in range(GROUP):
                first = (head * GROUP + i) * HEAD_FEATURES
                dq_ref[:, first : first + HEAD_FEATURES] = (
                    dq[:, i * tokens : (i + 1) * tokens].T.astype(BF16)
                )
            for block in range(back + 1):
                rows = dk[block * tokens : (block + 1) * tokens]
                dk_refs[block][:, columns] = rows.astype(dk_refs[block].dtype)

    out = pl.pallas_call(
        kernel,
        in_specs=[vmem()] * (2 * back + 5),
        out_specs=[vmem()] * (back + 2),
        out_shape=[jax.ShapeDtypeStruct(q.shape, BF16)]
        + [jax.ShapeDtypeStruct((tokens, kv), BF16)] * back
        + [jax.ShapeDtypeStruct((tokens, kv), F32)],
        compiler_params=params(),
        cost_estimate=SMALL,
        name="scores_grad",
    )(probs, q, o, *key_blocks, *value_blocks)
    return out[0], out[1:]


def swap(array, name):
    return flip(array, "seq", 1, name)


def x_halves_call(me, x, k, shards):
    tokens, model = x.shape
    half = model // shards // 2

    def kernel(me_ref, x_hbm, k_hbm, mine_ref, theirs_ref, k_ref, sems):
        core = me_ref[0] % 2
        pairs = [(k_hbm, k_ref)]
        for which, target in ((1 - core, theirs_ref), (core, mine_ref)):
            for shard in range(shards):
                first = pl.multiple_of(2 * shard * half + which * half, half)
                pairs.append(
                    (x_hbm.at[:, pl.ds(first, half)], target.at[:, pl.ds(shard * half, half)])
                )
        for copy in copies(pairs, sems):
            copy.wait()

    return pl.pallas_call(
        kernel,
        in_specs=[smem(), hbm(), hbm()],
        out_specs=[vmem()] * 3,
        out_shape=[jax.ShapeDtypeStruct((tokens, model // 2), BF16)] * 2
        + [jax.ShapeDtypeStruct(k.shape, BF16)],
        scratch_shapes=[dma(2 * shards + 1)],
        compiler_params=params(),
        cost_estimate=SMALL,
        name="x_halves",
    )(me, x, k)


def put_half_call(me, out, theirs, shards):
    tokens, model = out.shape
    half = model // shards // 2

    def kernel(me_ref, theirs_ref, out_in, out_hbm, sems):
        which = 1 - me_ref[0] % 2
        pairs = []
        for shard in range(shards):
            first = pl.multiple_of(2 * shard * half + which * half, half)
            pairs.append(
                (theirs_ref.at[:, pl.ds(shard * half, half)], out_hbm.at[:, pl.ds(first, half)])
            )
        for copy in copies(pairs, sems):
            copy.wait()

    return pl.pallas_call(
        kernel,
        in_specs=[smem(), vmem(), hbm()],
        out_specs=hbm(),
        out_shape=jax.ShapeDtypeStruct((tokens, model), BF16),
        scratch_shapes=[dma(shards)],
        input_output_aliases={2: 0},
        compiler_params=params(),
        cost_estimate=SMALL,
        name="put_half",
    )(me, theirs, out)


def join_call(me, mine, theirs, shards, model):
    rank, width = mine.shape
    kv = width - model // 2
    half = model // shards // 2

    def kernel(me_ref, mine_ref, theirs_ref, down_ref, up_ref):
        core = me_ref[0] % 2
        for which, ref in ((core, mine_ref), (1 - core, theirs_ref)):
            for shard in range(shards):
                first = pl.multiple_of(2 * shard * half + which * half, half)
                down_ref[:, pl.ds(first, half)] = ref[:, shard * half : (shard + 1) * half]
        up_ref[...] = mine_ref[:, model // 2 :] + theirs_ref[:, model // 2 :]

    return pl.pallas_call(
        kernel,
        in_specs=[smem(), vmem(), vmem()],
        out_specs=[vmem()] * 2,
        out_shape=[
            jax.ShapeDtypeStruct((rank, model), F32),
            jax.ShapeDtypeStruct((rank, kv), F32),
        ],
        compiler_params=params(),
        cost_estimate=SMALL,
        name="join_adapter",
    )(me, mine, theirs)


def own_values_call(me, x_mine, x_theirs, down, up, w):
    tokens, width = x_mine.shape
    rows, kv = w.shape
    rank, model = down.shape
    half = rows // 2
    shards = model // rows

    def kernel(me_ref, mine_ref, theirs_ref, down_ref, up_ref, w_ref, acc_ref, low_ref, down_half):
        core = me_ref[0] % 2
        for shard in range(shards):
            first = pl.multiple_of(shard * rows + core * half, half)
            down_half[:, shard * half : (shard + 1) * half] = down_ref[:, pl.ds(first, half)]
        x_rows = jnp.concatenate([mine_ref[...], theirs_ref[...]], axis=0)
        low = contract_trailing(x_rows, down_half[...])
        low_ref[...] = low
        adapter = jnp.dot(
            low,
            up_ref[...].astype(F32),
            precision=lax.Precision.HIGHEST,
            preferred_element_type=F32,
        )
        columns = pl.ds(pl.multiple_of(me_ref[1] * half, half), half)
        x_rows = jnp.concatenate([mine_ref[:, columns], theirs_ref[:, columns]], axis=0)
        own = w_ref[pl.ds(pl.multiple_of(core * half, half), half), :]
        acc_ref[...] = ADAPTER_SCALE * adapter + jnp.dot(x_rows, own, preferred_element_type=F32)

    return pl.pallas_call(
        kernel,
        in_specs=[smem()] + [vmem()] * 5,
        out_specs=[vmem()] * 2,
        out_shape=[
            jax.ShapeDtypeStruct((2 * tokens, kv), F32),
            jax.ShapeDtypeStruct((2 * tokens, rank), F32),
        ],
        scratch_shapes=[pltpu.VMEM((rank, width), BF16)],
        compiler_params=params(),
        cost_estimate=SMALL,
        name="own_values",
    )(me, x_mine, x_theirs, down, up, w)


class Pieces:
    def __init__(self, half, seq_count, fsdp_count):
        self.fsdp_count = fsdp_count
        self.half = half
        self.by_parts = (half // (seq_count // 2)) % 128 == 0
        self.step = half // (seq_count // 2) if self.by_parts else half
        self.each = half // self.step
        self.order = gather_order(seq_count)

    def chip(self, me_ref, number):
        if not self.by_parts:
            return 0
        even, odd = (int(self.order[i][number] ^ i) // 2 for i in range(2))
        here = me_ref[0]
        return lax.bitwise_xor(here // 2, jnp.where(here % 2 == 0, even, odd))

    def owner(self, me_ref, by):
        return lax.rem(me_ref[1] + (self.fsdp_count - by), self.fsdp_count)


def heights(arrays):
    firsts, first = [], 0
    for array in arrays:
        firsts.append(first)
        first += array.shape[0]
    return firsts, first


def more_values_call(me, x_mine, x_theirs, acc, shards, pieces, last):
    tokens = x_mine.shape[0]
    half, step = pieces.half, pieces.step
    bys = list(shards)
    arrays = [array for by in bys for array in shards[by]]
    firsts, _ = heights(arrays)
    kv = acc.shape[1]

    def kernel(me_ref, acc_ref, mine_ref, theirs_ref, *refs):
        outs = refs[len(arrays) :]
        mine, theirs = acc_ref[:tokens], acc_ref[tokens:]
        for ref, first, array in zip(refs, firsts, arrays):
            for row in range(0, array.shape[0], step):
                by, number = bys[(first + row) // half], (first + row) % half // step
                column = pieces.owner(me_ref, by) * half + pieces.chip(me_ref, number) * step
                columns = pl.ds(pl.multiple_of(column, step), step)
                x_rows = jnp.concatenate([mine_ref[:, columns], theirs_ref[:, columns]], axis=0)
                grown = jnp.dot(x_rows, ref[row : row + step, :], preferred_element_type=F32)
                mine, theirs = mine + grown[:tokens], theirs + grown[tokens:]
        if last:
            outs[0][...] = mine
            outs[1][...] = theirs
        else:
            outs[0][...] = jnp.concatenate([mine, theirs], axis=0)

    one = jax.ShapeDtypeStruct((tokens, kv), F32)
    out = pl.pallas_call(
        kernel,
        in_specs=[smem()] + [vmem()] * (3 + len(arrays)),
        out_specs=[vmem()] * (2 if last else 1),
        out_shape=[one, one] if last else [jax.ShapeDtypeStruct(acc.shape, F32)],
        compiler_params=params(),
        cost_estimate=SMALL,
        name="more_values",
    )(me, acc, x_mine, x_theirs, *arrays)
    return out if last else out[0]


def input_grad_call(me, dv_mine, dv_theirs, rank_grad, down, w, shards, pieces):
    tokens, kv = dv_mine.shape
    rank, model = down.shape
    half, step = pieces.half, pieces.step
    rows = 2 * half
    bys = list(shards)
    arrays = [array for by in bys for array in shards[by]]
    firsts, _ = heights(arrays)
    count = 1 + len(bys)
    width = model // 2

    def kernel(me_ref, mine_ref, theirs_ref, rank_ref, down_ref, w_ref, *refs):
        out_hbm, send_hbm, down_half, term, buffer, out_sems = refs[len(arrays) :]
        core = me_ref[0] % 2
        starts = [pl.multiple_of(i * rows + core * half, half) for i in range(count)]
        for i in range(count):
            down_half[:, i * half : (i + 1) * half] = down_ref[:, pl.ds(starts[i], half)]
        term[...] = jnp.dot(rank_ref[...], down_half[...], preferred_element_type=F32)
        dv = jnp.concatenate([mine_ref[...], theirs_ref[...]], axis=0)
        own = pl.ds(pl.multiple_of(me_ref[1] * half, half), half)
        own_rows_of_w = pl.ds(pl.multiple_of(core * half, half), half)
        buffer[:, own] = (contract_trailing(dv, w_ref[own_rows_of_w, :]) + term[:, own]).astype(BF16)
        for ref, first, array in zip(refs, firsts, arrays):
            for row in range(0, array.shape[0], step):
                by, number = bys[(first + row) // half], (first + row) % half // step
                column = pieces.owner(me_ref, by) * half + pieces.chip(me_ref, number) * step
                columns = pl.ds(pl.multiple_of(column, step), step)
                grad = contract_trailing(dv, ref[row : row + step, :]) + term[:, columns]
                buffer[:, columns] = grad.astype(BF16)
        pairs = [(buffer.at[pl.ds(tokens, tokens)], send_hbm)]
        for i in range(count):
            pairs.append(
                (
                    buffer.at[pl.ds(0, tokens), pl.ds(i * half, half)],
                    out_hbm.at[:, pl.ds(starts[i], half)],
                )
            )
        for copy in copies(pairs, out_sems):
            copy.wait()

    return pl.pallas_call(
        kernel,
        in_specs=[smem()] + [vmem()] * (5 + len(arrays)),
        out_specs=[hbm()] * 2,
        out_shape=[
            jax.ShapeDtypeStruct((tokens, model), BF16),
            jax.ShapeDtypeStruct((tokens, width), BF16),
        ],
        scratch_shapes=[
            pltpu.VMEM((rank, width), BF16),
            pltpu.VMEM((2 * tokens, width), F32),
            pltpu.VMEM((2 * tokens, width), BF16),
            dma(1 + count),
        ],
        compiler_params=params(),
        cost_estimate=SMALL,
        name="input_grad",
    )(me, dv_mine, dv_theirs, rank_grad, down, w, *arrays)


def adapter_grad_call(dv_mine, dv_theirs, up, low, x_mine, x_theirs, scale):
    tokens, width = x_mine.shape
    rank, kv = up.shape

    def kernel(mine_ref, theirs_ref, up_ref, low_ref, x_mine_ref, x_theirs_ref, rank_ref, out_ref):
        dv = jnp.concatenate([mine_ref[...], theirs_ref[...]], axis=0)
        rank_low = (ADAPTER_SCALE * contract_trailing(dv, up_ref[...])).astype(BF16)
        rank_ref[...] = rank_low
        raised = contract_leading(low_ref[...], dv.astype(F32), lax.Precision.HIGHEST)
        out_ref[:, width:] = (raised * (ADAPTER_SCALE * scale)).astype(BF16)
        x_rows = jnp.concatenate([x_mine_ref[...], x_theirs_ref[...]], axis=0)
        out_ref[:, :width] = (contract_leading(rank_low, x_rows) * scale).astype(BF16)

    return pl.pallas_call(
        kernel,
        in_specs=[vmem()] * 6,
        out_specs=[vmem()] * 2,
        out_shape=[
            jax.ShapeDtypeStruct((2 * tokens, rank), BF16),
            jax.ShapeDtypeStruct((rank, width + kv), BF16),
        ],
        compiler_params=params(),
        cost_estimate=SMALL,
        name="adapter_grad",
    )(dv_mine, dv_theirs, up, low, x_mine, x_theirs)


def sum_steps(seq_count, fsdp_count):
    ring = [("fsdp", 1 << b) for b in range(fsdp_count.bit_length() - 1)]
    chips = [("seq", bit) for bit in chip_bits(seq_count)[::-1]]
    steps = []
    while ring or chips:
        steps += ring[:1] + chips[:1]
        ring, chips = ring[1:], chips[1:]
    return steps


def sum_step(low, step, keep=False):
    axis, mask = step
    total = low.astype(F32) + flip(low, axis, mask, "adapter_sum").astype(F32)
    return total if keep else total.astype(BF16)


def chip_bits(seq_count):
    return [1 << b for b in range(1, seq_count.bit_length() - 1)]


def chip_mask(seq_count, stage):
    bits = chip_bits(seq_count)
    return lambda index: bits[stage] if index % 2 == 0 else bits[len(bits) - 1 - stage]


def gather_order(seq_count):
    held = [[i] for i in range(seq_count)]
    for stage in range(len(chip_bits(seq_count))):
        mask = chip_mask(seq_count, stage)
        held = [held[i] + held[i ^ mask(i)] for i in range(seq_count)]
    order = np.array(held, np.int32)
    relative = order ^ np.arange(seq_count, dtype=np.int32)[:, None]
    assert (relative == relative[np.arange(seq_count) % 2]).all()
    return order


def ring_order(fsdp_count):
    return sorted(range(1, fsdp_count), key=lambda by: (min(by, fsdp_count - by), by))


def across(array, stage):
    mask = chip_mask(lax.axis_size("seq"), stage)
    return flip(array, "seq", mask, f"weight_chip_{stage}")


def spread_step(held):
    stages = len(chip_bits(lax.axis_size("seq")))
    size = len(held)
    if size == 1 << stages:
        return None
    if size == 1 and stages >= 2:
        return held + [across(held[0], 0), across(held[0], 1)]
    if size == 3:
        return held + [across(held[1], 1)]
    stage = size.bit_length() - 1
    if size == 1:
        return held + [across(held[0], stage)]
    joined = jnp.concatenate(held, axis=0)
    other = across(joined, stage)
    height = held[0].shape[0]
    return held + [other[i * height : (i + 1) * height] for i in range(size)]


def natural_half(held, order, here):
    width = held[0].shape[1]
    chips = jnp.asarray(order)[here] // 2
    joined = jnp.concatenate(held, axis=0).reshape(len(held), -1, width)
    return [jnp.take(joined, jnp.argsort(chips), axis=0).reshape(-1, width)]


def body(
    normed_block_input,
    stored_rotated_queries,
    stored_rotated_keys,
    attention_output_gradient,
    frozen_value_weight,
    adapter_down_weight,
    adapter_up_weight,
    packed_document_lengths,
):
    x = normed_block_input[0]
    q = stored_rotated_queries[0]
    k = stored_rotated_keys[0]
    o = attention_output_gradient[0]
    w = frozen_value_weight
    down, up = adapter_down_weight, adapter_up_weight
    tokens, model = x.shape
    seq_count = lax.axis_size("seq")
    fsdp_count = lax.axis_size("fsdp")
    here = lax.axis_index("seq")
    half = w.shape[0] // 2
    part_rows = half // (seq_count // 2)
    longest = tokens * seq_count // 4
    back = -(-longest // tokens)
    me = jnp.concatenate(
        [jnp.stack([here, lax.axis_index("fsdp")]), packed_document_lengths[0]]
    ).astype(jnp.int32)
    pieces = Pieces(half, seq_count, fsdp_count)
    ring = ring_order(fsdp_count)

    chips = seq_count // 2
    direct = chips == 4

    def part_of(chip):
        first_row = (here % 2) * half + chip * part_rows
        return lax.dynamic_slice_in_dim(w, first_row, part_rows, 0)

    def ring_step(known, bys, name):
        for by in bys:
            upward = 2 * by <= fsdp_count
            source = by - 1 if upward else (by + 1) % fsdp_count
            known[by] = turn(known[source], "fsdp", 1 if upward else -1, name)

    def set_out(bys):
        for by in bys:
            held[by] = spread_step([arrived[by]]) or [arrived[by]]

    held = {}
    arrived = {0: part_of(here // 2)}
    across = {0: part_of(here // 2 ^ 3)} if direct else {}

    ring_step(arrived, ring[:2], "weight_ring")
    arrived[0], x = after((arrived[0], x))
    key_blocks = [shift(k, "seq", by, "key_halo") for by in range(back, 0, -1)]
    x_mine, x_sent, k = x_halves_call(me, x, k, fsdp_count)
    key_blocks.append(k)
    probs, dv_blocks = probs_call(me, q, o, key_blocks)
    arrived, across, dv_blocks, x_mine, x_sent = after(
        (arrived, across, dv_blocks, x_mine, x_sent)
    )

    dv_back = [
        shift(dv_blocks[back - by], "seq", -by, "value_grad_halo") for by in range(1, back + 1)
    ]
    ring_step(arrived, ring[2:], "weight_ring")
    if direct:
        set_out(ring[:1])
    x_theirs = swap(x_sent, "x_core")
    acc, low = own_values_call(me, x_mine, x_theirs, down, up, w)
    held, arrived, dv_back, acc, low = after((held, arrived, dv_back, acc, low))

    if direct:
        set_out(ring[1:2])
        ring_step(across, ring[:1], "weight_ring_across")
    dv = dv_blocks[back]
    for block in dv_back:
        dv = dv + block.astype(F32)
    dv_mine = dv.astype(BF16)
    dv_theirs = swap(dv_mine, "value_grad_core")
    scale = 1.0 / (tokens * seq_count * fsdp_count)
    rank_grad, sums = adapter_grad_call(dv_mine, dv_theirs, up, low, x_mine, x_theirs, scale)
    across, held, sums = after((across, held, sums))

    steps = sum_steps(seq_count, fsdp_count)
    if direct:
        set_out(ring[2:])
        ring_step(across, ring[2:], "weight_ring_across")
        held = {
            by: held[by] + [across[by]] if by in across else spread_step(held[by]) for by in ring
        }
    else:
        set_out(ring)
    if len(steps) > 3:
        sums = sum_step(sums, steps.pop(0))
    held, acc, sums = after((held, acc, sums))
    while any(len(parts) < chips for parts in held.values()):
        held = after({by: spread_step(parts) for by, parts in held.items()})

    def arrays_of(parts):
        if pieces.by_parts:
            return parts
        return {by: natural_half(parts[by], pieces.order, here) for by in parts}

    if len(steps) > 2:
        sums = sum_step(sums, steps.pop(0))
    values, values_sent = more_values_call(
        me, x_mine, x_theirs, acc, arrays_of(held), pieces, True
    )

    values = (values + swap(values_sent, "values_core")).astype(BF16)
    values, dv_mine, sums = after((values, dv_mine, sums))
    value_blocks = [shift(values, "seq", by, "value_halo") for by in range(back, 0, -1)] + [values]
    while len(steps) > 1:
        sums = sum_step(sums, steps.pop(0))
    input_grad, input_grad_sent = input_grad_call(
        me, dv_mine, dv_theirs, rank_grad, down, w, arrays_of(held), pieces
    )
    value_blocks, sums, input_grad_sent = after((value_blocks, sums, input_grad_sent))

    total = sum_step(sums, steps[0], keep=True) if steps else sums.astype(F32)
    rotated_query_gradient, dk_blocks = scores_grad_call(probs, q, o, key_blocks, value_blocks)
    total, input_grad_sent, dk_blocks = after((total, input_grad_sent, dk_blocks))
    dk_back = [
        shift(dk_blocks[back - by], "seq", -by, "key_grad_halo") for by in range(1, back + 1)
    ]
    total_theirs = swap(total, "adapter_core")
    input_grad_theirs = swap(input_grad_sent, "input_grad_core")
    input_gradient = put_half_call(me, input_grad, input_grad_theirs, fsdp_count)
    down_gradient, up_gradient = join_call(me, total, total_theirs, fsdp_count, model)
    dk_back, input_gradient, down_gradient, up_gradient = after(
        (dk_back, input_gradient, down_gradient, up_gradient)
    )
    key_gradient = dk_blocks[back]
    for block in dk_back:
        key_gradient = key_gradient + block.astype(F32)
    return (
        input_gradient[None],
        rotated_query_gradient[None],
        key_gradient.astype(BF16)[None],
        down_gradient,
        up_gradient,
    )


def solution(mesh):
    placed = (
        P("fsdp", "seq", None),
        P("fsdp", "seq", None),
        P("fsdp", "seq", None),
        P("fsdp", "seq", None),
        P("fsdp", None),
        P(),
        P(),
        P("fsdp", None),
    )
    return jax.shard_map(
        body,
        mesh=mesh,
        in_specs=placed,
        out_specs=(
            P("fsdp", "seq", None),
            P("fsdp", "seq", None),
            P("fsdp", "seq", None),
            P(),
            P(),
        ),
        check_vma=False,
    )
```

```python
import math

import jax
import jax.numpy as jnp
import numpy as np
from jax import lax
from jax.experimental import pallas as pl
from jax.experimental.pallas import tpu as pltpu
from jax.sharding import PartitionSpec as P

HEAD_FEATURES = 128
QUERY_HEADS = 32
KEY_VALUE_HEADS = 4
GROUP = QUERY_HEADS // KEY_VALUE_HEADS
ADAPTER_SCALE = 2.0
NEG_FILL = -1e30
INVERSE = HEAD_FEATURES ** (-0.5)
LOG2E = math.log2(math.e)
VMEM_LIMIT = 32 * 1024 * 1024
SMALL = pl.CostEstimate(flops=1, bytes_accessed=1, transcendentals=0)
F32 = jnp.float32
BF16 = jnp.bfloat16


def params():
    return pltpu.CompilerParams(vmem_limit_bytes=VMEM_LIMIT)


def contract_trailing(left, right):
    return lax.dot_general(left, right, (((1,), (1,)), ((), ())), preferred_element_type=F32)


def contract_leading(left, right, precision=None):
    return lax.dot_general(
        left, right, (((0,), (0,)), ((), ())), preferred_element_type=F32, precision=precision
    )


def flip(value, axis, mask, name="exchange"):
    size = lax.axis_size(axis)
    choose = mask if callable(mask) else (lambda index: mask)
    with jax.named_scope(name):
        return lax.ppermute(value, axis, [(i, i ^ choose(i)) for i in range(size)])


def shift(value, axis, by, name="halo"):
    size = lax.axis_size(axis)
    with jax.named_scope(name):
        return lax.ppermute(value, axis, [(i, i + by) for i in range(size) if 0 <= i + by < size])


def turn(value, axis, by, name="weight_ring"):
    size = lax.axis_size(axis)
    with jax.named_scope(name):
        return lax.ppermute(value, axis, [(i, (i + by) % size) for i in range(size)])


def after(values):
    return lax.optimization_barrier(values)


def vmem():
    return pl.BlockSpec(memory_space=pltpu.VMEM)


def smem():
    return pl.BlockSpec(memory_space=pltpu.SMEM)


def hbm():
    return pl.BlockSpec(memory_space=pltpu.HBM)


def copies(pairs, sems):
    started = []
    for number, (source, target) in enumerate(pairs):
        copy = pltpu.make_async_copy(source, target, sems.at[number])
        copy.start()
        started.append(copy)
    return started


def dma(count):
    return pltpu.SemaphoreType.DMA((count,))


def column_blocks(ref, count):
    width = ref.shape[1] // count
    return [ref.at[:, pl.ds(i * width, width)] for i in range(count)]


def head_rows(ref, head):
    first = head * GROUP
    return jnp.concatenate(
        [
            ref[:, (first + i) * HEAD_FEATURES : (first + i + 1) * HEAD_FEATURES]
            for i in range(GROUP)
        ],
        axis=0,
    )


def own_rows(tokens):
    key = lax.broadcasted_iota(jnp.int32, (tokens, GROUP * tokens), 0)
    query = lax.broadcasted_iota(jnp.int32, (tokens, GROUP * tokens), 1) % tokens
    return key <= query


def to_slots(rows, own, tokens):
    last = rows.shape[0] - tokens
    return jnp.concatenate(
        [jnp.where(own, rows[last:], rows[:tokens]), rows[tokens:last]], axis=0
    )


def from_slots(slots, own, tokens):
    shared = slots[:tokens]
    return jnp.concatenate(
        [
            jnp.where(own, 0.0, shared).astype(BF16),
            slots[tokens:].astype(BF16),
            jnp.where(own, shared, 0.0).astype(BF16),
        ],
        axis=0,
    )


def probs_call(me, q, o, key_blocks):
    back = len(key_blocks) - 1
    docs = me.shape[0] - 2
    tokens = q.shape[0]
    kv = key_blocks[0].shape[1]
    slots = back * tokens

    def kernel(me_ref, q_ref, o_ref, *refs):
        key_refs = refs[: back + 1]
        p_ref = refs[back + 1]
        dv_refs = refs[back + 2 : 2 * back + 3]
        bias_ref = refs[2 * back + 3]

        def fill_bias():
            here = me_ref[0]
            key = lax.broadcasted_iota(jnp.int32, (slots, tokens), 0)
            query = lax.broadcasted_iota(jnp.int32, (slots, tokens), 1)
            query_place = here * tokens + query
            shared = (key < tokens) & (key <= query)
            key_place = here * tokens + jnp.where(shared, key, key - slots)
            opening = jnp.zeros((slots, tokens), jnp.int32)
            bound = jnp.int32(0)
            for doc in range(docs):
                bound = bound + me_ref[2 + doc]
                opening = jnp.where(query_place >= bound, bound, opening)
            bias_ref[...] = jnp.where(key_place >= opening, 0.0, NEG_FILL)

        fill_bias()
        own = own_rows(tokens)
        for head in range(KEY_VALUE_HEADS):
            columns = slice(head * HEAD_FEATURES, (head + 1) * HEAD_FEATURES)
            key_rows = jnp.concatenate([r[:, columns] for r in key_refs], axis=0)
            scores = contract_trailing(key_rows, head_rows(q_ref, head))
            scores = to_slots(scores, own, tokens)
            scores = scores + jnp.concatenate([bias_ref[...]] * GROUP, axis=1)
            peak = jnp.max(scores, axis=0, keepdims=True)
            weights = jnp.exp2((scores - peak) * (INVERSE * LOG2E))
            probs = weights * (1.0 / jnp.sum(weights, axis=0, keepdims=True))
            p_ref[head] = probs.astype(BF16)
            dv = jnp.dot(
                from_slots(probs, own, tokens),
                head_rows(o_ref, head),
                preferred_element_type=F32,
            )
            for block in range(back + 1):
                rows = dv[block * tokens : (block + 1) * tokens]
                dv_refs[block][:, columns] = rows.astype(dv_refs[block].dtype)

    out = pl.pallas_call(
        kernel,
        in_specs=[smem()] + [vmem()] * (back + 3),
        out_specs=[vmem()] * (back + 2),
        out_shape=[jax.ShapeDtypeStruct((KEY_VALUE_HEADS, slots, GROUP * tokens), BF16)]
        + [jax.ShapeDtypeStruct((tokens, kv), BF16)] * back
        + [jax.ShapeDtypeStruct((tokens, kv), F32)],
        scratch_shapes=[pltpu.VMEM((slots, tokens), F32)],
        compiler_params=params(),
        cost_estimate=SMALL,
        name="probs",
    )(me, q, o, *key_blocks)
    return out[0], out[1:]


def scores_grad_call(probs, q, o, key_blocks, value_blocks):
    back = len(key_blocks) - 1
    tokens = q.shape[0]
    kv = key_blocks[0].shape[1]

    def kernel(p_ref, q_ref, o_ref, *refs):
        key_refs = refs[: back + 1]
        value_refs = refs[back + 1 : 2 * back + 2]
        dq_ref = refs[2 * back + 2]
        dk_refs = refs[2 * back + 3 :]
        own = own_rows(tokens)
        for head in range(KEY_VALUE_HEADS):
            columns = slice(head * HEAD_FEATURES, (head + 1) * HEAD_FEATURES)
            key_rows = jnp.concatenate([r[:, columns] for r in key_refs], axis=0)
            value_rows = jnp.concatenate([r[:, columns] for r in value_refs], axis=0)
            grad_probs = contract_trailing(value_rows, head_rows(o_ref, head))
            grad_probs = to_slots(grad_probs, own, tokens)
            probs = p_ref[head].astype(F32)
            mass = jnp.sum(probs, axis=0, keepdims=True)
            delta = jnp.sum(probs * grad_probs, axis=0, keepdims=True) / mass
            grad_scores = from_slots(probs * (grad_probs - delta), own, tokens)
            dk = jnp.dot(grad_scores, head_rows(q_ref, head), preferred_element_type=F32)
            dk = dk * INVERSE
            dq = jnp.dot(key_rows.T, grad_scores, preferred_element_type=F32) * INVERSE
            for i in range(GROUP):
                first = (head * GROUP + i) * HEAD_FEATURES
                dq_ref[:, first : first + HEAD_FEATURES] = (
                    dq[:, i * tokens : (i + 1) * tokens].T.astype(BF16)
                )
            for block in range(back + 1):
                rows = dk[block * tokens : (block + 1) * tokens]
                dk_refs[block][:, columns] = rows.astype(dk_refs[block].dtype)

    out = pl.pallas_call(
        kernel,
        in_specs=[vmem()] * (2 * back + 5),
        out_specs=[vmem()] * (back + 2),
        out_shape=[jax.ShapeDtypeStruct(q.shape, BF16)]
        + [jax.ShapeDtypeStruct((tokens, kv), BF16)] * back
        + [jax.ShapeDtypeStruct((tokens, kv), F32)],
        compiler_params=params(),
        cost_estimate=SMALL,
        name="scores_grad",
    )(probs, q, o, *key_blocks, *value_blocks)
    return out[0], out[1:]


def swap(array, name):
    return flip(array, "seq", 1, name)


def x_halves_call(me, x, k, shards):
    tokens, model = x.shape
    half = model // shards // 2

    def kernel(me_ref, x_hbm, k_hbm, mine_ref, theirs_ref, k_ref, sems):
        core = me_ref[0] % 2
        pairs = [(k_hbm, k_ref)]
        for which, target in ((1 - core, theirs_ref), (core, mine_ref)):
            for shard in range(shards):
                first = pl.multiple_of(2 * shard * half + which * half, half)
                pairs.append(
                    (x_hbm.at[:, pl.ds(first, half)], target.at[:, pl.ds(shard * half, half)])
                )
        for copy in copies(pairs, sems):
            copy.wait()

    return pl.pallas_call(
        kernel,
        in_specs=[smem(), hbm(), hbm()],
        out_specs=[vmem()] * 3,
        out_shape=[jax.ShapeDtypeStruct((tokens, model // 2), BF16)] * 2
        + [jax.ShapeDtypeStruct(k.shape, BF16)],
        scratch_shapes=[dma(2 * shards + 1)],
        compiler_params=params(),
        cost_estimate=SMALL,
        name="x_halves",
    )(me, x, k)


def put_half_call(me, out, theirs, shards):
    tokens, model = out.shape
    half = model // shards // 2

    def kernel(me_ref, theirs_ref, out_in, out_hbm, sems):
        which = 1 - me_ref[0] % 2
        pairs = []
        for shard in range(shards):
            first = pl.multiple_of(2 * shard * half + which * half, half)
            pairs.append(
                (theirs_ref.at[:, pl.ds(shard * half, half)], out_hbm.at[:, pl.ds(first, half)])
            )
        for copy in copies(pairs, sems):
            copy.wait()

    return pl.pallas_call(
        kernel,
        in_specs=[smem(), vmem(), hbm()],
        out_specs=hbm(),
        out_shape=jax.ShapeDtypeStruct((tokens, model), BF16),
        scratch_shapes=[dma(shards)],
        input_output_aliases={2: 0},
        compiler_params=params(),
        cost_estimate=SMALL,
        name="put_half",
    )(me, theirs, out)


def join_call(me, mine, theirs, shards, model):
    rank, width = mine.shape
    kv = width - model // 2
    half = model // shards // 2

    def kernel(me_ref, mine_ref, theirs_ref, down_ref, up_ref):
        core = me_ref[0] % 2
        for which, ref in ((core, mine_ref), (1 - core, theirs_ref)):
            for shard in range(shards):
                first = pl.multiple_of(2 * shard * half + which * half, half)
                down_ref[:, pl.ds(first, half)] = ref[:, shard * half : (shard + 1) * half]
        up_ref[...] = mine_ref[:, model // 2 :] + theirs_ref[:, model // 2 :]

    return pl.pallas_call(
        kernel,
        in_specs=[smem(), vmem(), vmem()],
        out_specs=[vmem()] * 2,
        out_shape=[
            jax.ShapeDtypeStruct((rank, model), F32),
            jax.ShapeDtypeStruct((rank, kv), F32),
        ],
        compiler_params=params(),
        cost_estimate=SMALL,
        name="join_adapter",
    )(me, mine, theirs)


def own_values_call(me, x_mine, x_theirs, down, up, w):
    tokens, width = x_mine.shape
    rows, kv = w.shape
    rank, model = down.shape
    half = rows // 2
    shards = model // rows

    def kernel(me_ref, mine_ref, theirs_ref, down_ref, up_ref, w_ref, acc_ref, low_ref, down_half):
        core = me_ref[0] % 2
        for shard in range(shards):
            first = pl.multiple_of(shard * rows + core * half, half)
            down_half[:, shard * half : (shard + 1) * half] = down_ref[:, pl.ds(first, half)]
        x_rows = jnp.concatenate([mine_ref[...], theirs_ref[...]], axis=0)
        low = contract_trailing(x_rows, down_half[...])
        low_ref[...] = low
        adapter = jnp.dot(
            low,
            up_ref[...].astype(F32),
            precision=lax.Precision.HIGHEST,
            preferred_element_type=F32,
        )
        columns = pl.ds(pl.multiple_of(me_ref[1] * half, half), half)
        x_rows = jnp.concatenate([mine_ref[:, columns], theirs_ref[:, columns]], axis=0)
        own = w_ref[pl.ds(pl.multiple_of(core * half, half), half), :]
        acc_ref[...] = ADAPTER_SCALE * adapter + jnp.dot(x_rows, own, preferred_element_type=F32)

    return pl.pallas_call(
        kernel,
        in_specs=[smem()] + [vmem()] * 5,
        out_specs=[vmem()] * 2,
        out_shape=[
            jax.ShapeDtypeStruct((2 * tokens, kv), F32),
            jax.ShapeDtypeStruct((2 * tokens, rank), F32),
        ],
        scratch_shapes=[pltpu.VMEM((rank, width), BF16)],
        compiler_params=params(),
        cost_estimate=SMALL,
        name="own_values",
    )(me, x_mine, x_theirs, down, up, w)


class Pieces:
    def __init__(self, half, seq_count, fsdp_count):
        self.fsdp_count = fsdp_count
        self.half = half
        self.by_parts = (half // (seq_count // 2)) % 128 == 0
        self.step = half // (seq_count // 2) if self.by_parts else half
        self.each = half // self.step
        self.order = gather_order(seq_count)

    def chip(self, me_ref, number):
        if not self.by_parts:
            return 0
        even, odd = (int(self.order[i][number] ^ i) // 2 for i in range(2))
        here = me_ref[0]
        return lax.bitwise_xor(here // 2, jnp.where(here % 2 == 0, even, odd))

    def owner(self, me_ref, by):
        return lax.rem(me_ref[1] + (self.fsdp_count - by), self.fsdp_count)


def heights(arrays):
    firsts, first = [], 0
    for array in arrays:
        firsts.append(first)
        first += array.shape[0]
    return firsts, first


def more_values_call(me, x_mine, x_theirs, acc, shards, pieces, last):
    tokens = x_mine.shape[0]
    half, step = pieces.half, pieces.step
    bys = list(shards)
    arrays = [array for by in bys for array in shards[by]]
    firsts, _ = heights(arrays)
    kv = acc.shape[1]

    def kernel(me_ref, acc_ref, mine_ref, theirs_ref, *refs):
        outs = refs[len(arrays) :]
        mine, theirs = acc_ref[:tokens], acc_ref[tokens:]
        for ref, first, array in zip(refs, firsts, arrays):
            for row in range(0, array.shape[0], step):
                by, number = bys[(first + row) // half], (first + row) % half // step
                column = pieces.owner(me_ref, by) * half + pieces.chip(me_ref, number) * step
                columns = pl.ds(pl.multiple_of(column, step), step)
                x_rows = jnp.concatenate([mine_ref[:, columns], theirs_ref[:, columns]], axis=0)
                grown = jnp.dot(x_rows, ref[row : row + step, :], preferred_element_type=F32)
                mine, theirs = mine + grown[:tokens], theirs + grown[tokens:]
        if last:
            outs[0][...] = mine
            outs[1][...] = theirs
        else:
            outs[0][...] = jnp.concatenate([mine, theirs], axis=0)

    one = jax.ShapeDtypeStruct((tokens, kv), F32)
    out = pl.pallas_call(
        kernel,
        in_specs=[smem()] + [vmem()] * (3 + len(arrays)),
        out_specs=[vmem()] * (2 if last else 1),
        out_shape=[one, one] if last else [jax.ShapeDtypeStruct(acc.shape, F32)],
        compiler_params=params(),
        cost_estimate=SMALL,
        name="more_values",
    )(me, acc, x_mine, x_theirs, *arrays)
    return out if last else out[0]


def input_grad_call(me, dv_mine, dv_theirs, rank_grad, down, w, shards, pieces):
    tokens, kv = dv_mine.shape
    rank, model = down.shape
    half, step = pieces.half, pieces.step
    rows = 2 * half
    bys = list(shards)
    arrays = [array for by in bys for array in shards[by]]
    firsts, _ = heights(arrays)
    count = 1 + len(bys)
    width = model // 2

    def kernel(me_ref, mine_ref, theirs_ref, rank_ref, down_ref, w_ref, *refs):
        out_hbm, send_hbm, down_half, term, buffer, out_sems = refs[len(arrays) :]
        core = me_ref[0] % 2
        starts = [pl.multiple_of(i * rows + core * half, half) for i in range(count)]
        for i in range(count):
            down_half[:, i * half : (i + 1) * half] = down_ref[:, pl.ds(starts[i], half)]
        term[...] = jnp.dot(rank_ref[...], down_half[...], preferred_element_type=F32)
        dv = jnp.concatenate([mine_ref[...], theirs_ref[...]], axis=0)
        own = pl.ds(pl.multiple_of(me_ref[1] * half, half), half)
        own_rows_of_w = pl.ds(pl.multiple_of(core * half, half), half)
        buffer[:, own] = (contract_trailing(dv, w_ref[own_rows_of_w, :]) + term[:, own]).astype(BF16)
        for ref, first, array in zip(refs, firsts, arrays):
            for row in range(0, array.shape[0], step):
                by, number = bys[(first + row) // half], (first + row) % half // step
                column = pieces.owner(me_ref, by) * half + pieces.chip(me_ref, number) * step
                columns = pl.ds(pl.multiple_of(column, step), step)
                grad = contract_trailing(dv, ref[row : row + step, :]) + term[:, columns]
                buffer[:, columns] = grad.astype(BF16)
        pairs = [(buffer.at[pl.ds(tokens, tokens)], send_hbm)]
        for i in range(count):
            pairs.append(
                (
                    buffer.at[pl.ds(0, tokens), pl.ds(i * half, half)],
                    out_hbm.at[:, pl.ds(starts[i], half)],
                )
            )
        for copy in copies(pairs, out_sems):
            copy.wait()

    return pl.pallas_call(
        kernel,
        in_specs=[smem()] + [vmem()] * (5 + len(arrays)),
        out_specs=[hbm()] * 2,
        out_shape=[
            jax.ShapeDtypeStruct((tokens, model), BF16),
            jax.ShapeDtypeStruct((tokens, width), BF16),
        ],
        scratch_shapes=[
            pltpu.VMEM((rank, width), BF16),
            pltpu.VMEM((2 * tokens, width), F32),
            pltpu.VMEM((2 * tokens, width), BF16),
            dma(1 + count),
        ],
        compiler_params=params(),
        cost_estimate=SMALL,
        name="input_grad",
    )(me, dv_mine, dv_theirs, rank_grad, down, w, *arrays)


def adapter_grad_call(dv_mine, dv_theirs, up, low, x_mine, x_theirs, scale):
    tokens, width = x_mine.shape
    rank, kv = up.shape

    def kernel(mine_ref, theirs_ref, up_ref, low_ref, x_mine_ref, x_theirs_ref, rank_ref, out_ref):
        dv = jnp.concatenate([mine_ref[...], theirs_ref[...]], axis=0)
        rank_low = (ADAPTER_SCALE * contract_trailing(dv, up_ref[...])).astype(BF16)
        rank_ref[...] = rank_low
        raised = contract_leading(low_ref[...], dv.astype(F32), lax.Precision.HIGHEST)
        out_ref[:, width:] = (raised * (ADAPTER_SCALE * scale)).astype(BF16)
        x_rows = jnp.concatenate([x_mine_ref[...], x_theirs_ref[...]], axis=0)
        out_ref[:, :width] = (contract_leading(rank_low, x_rows) * scale).astype(BF16)

    return pl.pallas_call(
        kernel,
        in_specs=[vmem()] * 6,
        out_specs=[vmem()] * 2,
        out_shape=[
            jax.ShapeDtypeStruct((2 * tokens, rank), BF16),
            jax.ShapeDtypeStruct((rank, width + kv), BF16),
        ],
        compiler_params=params(),
        cost_estimate=SMALL,
        name="adapter_grad",
    )(dv_mine, dv_theirs, up, low, x_mine, x_theirs)


def sum_steps(seq_count, fsdp_count):
    ring = [("fsdp", 1 << b) for b in range(fsdp_count.bit_length() - 1)]
    chips = [("seq", bit) for bit in chip_bits(seq_count)[::-1]]
    steps = []
    while ring or chips:
        steps += ring[:1] + chips[:1]
        ring, chips = ring[1:], chips[1:]
    return steps


def sum_step(low, step, keep=False):
    axis, mask = step
    total = low.astype(F32) + flip(low, axis, mask, "adapter_sum").astype(F32)
    return total if keep else total.astype(BF16)


def chip_bits(seq_count):
    return [1 << b for b in range(1, seq_count.bit_length() - 1)]


def chip_mask(seq_count, stage):
    bits = chip_bits(seq_count)
    return lambda index: bits[stage] if index % 2 == 0 else bits[len(bits) - 1 - stage]


def gather_order(seq_count):
    held = [[i] for i in range(seq_count)]
    for stage in range(len(chip_bits(seq_count))):
        mask = chip_mask(seq_count, stage)
        held = [held[i] + held[i ^ mask(i)] for i in range(seq_count)]
    order = np.array(held, np.int32)
    relative = order ^ np.arange(seq_count, dtype=np.int32)[:, None]
    assert (relative == relative[np.arange(seq_count) % 2]).all()
    return order


def ring_order(fsdp_count):
    return sorted(range(1, fsdp_count), key=lambda by: (min(by, fsdp_count - by), by))


def across(array, stage):
    mask = chip_mask(lax.axis_size("seq"), stage)
    return flip(array, "seq", mask, f"weight_chip_{stage}")


def spread_step(held):
    stages = len(chip_bits(lax.axis_size("seq")))
    size = len(held)
    if size == 1 << stages:
        return None
    if size == 1 and stages >= 2:
        return held + [across(held[0], 0), across(held[0], 1)]
    if size == 3:
        return held + [across(held[1], 1)]
    stage = size.bit_length() - 1
    if size == 1:
        return held + [across(held[0], stage)]
    joined = jnp.concatenate(held, axis=0)
    other = across(joined, stage)
    height = held[0].shape[0]
    return held + [other[i * height : (i + 1) * height] for i in range(size)]


def natural_half(held, order, here):
    width = held[0].shape[1]
    chips = jnp.asarray(order)[here] // 2
    joined = jnp.concatenate(held, axis=0).reshape(len(held), -1, width)
    return [jnp.take(joined, jnp.argsort(chips), axis=0).reshape(-1, width)]


def body(
    normed_block_input,
    stored_rotated_queries,
    stored_rotated_keys,
    attention_output_gradient,
    frozen_value_weight,
    adapter_down_weight,
    adapter_up_weight,
    packed_document_lengths,
):
    x = normed_block_input[0]
    q = stored_rotated_queries[0]
    k = stored_rotated_keys[0]
    o = attention_output_gradient[0]
    w = frozen_value_weight
    down, up = adapter_down_weight, adapter_up_weight
    tokens, model = x.shape
    seq_count = lax.axis_size("seq")
    fsdp_count = lax.axis_size("fsdp")
    here = lax.axis_index("seq")
    half = w.shape[0] // 2
    part_rows = half // (seq_count // 2)
    longest = tokens * seq_count // 4
    back = -(-longest // tokens)
    me = jnp.concatenate(
        [jnp.stack([here, lax.axis_index("fsdp")]), packed_document_lengths[0]]
    ).astype(jnp.int32)
    pieces = Pieces(half, seq_count, fsdp_count)
    ring = ring_order(fsdp_count)

    chips = seq_count // 2
    direct = chips == 4

    def part_of(chip):
        first_row = (here % 2) * half + chip * part_rows
        return lax.dynamic_slice_in_dim(w, first_row, part_rows, 0)

    def ring_step(known, bys, name):
        for by in bys:
            upward = 2 * by <= fsdp_count
            source = by - 1 if upward else (by + 1) % fsdp_count
            known[by] = turn(known[source], "fsdp", 1 if upward else -1, name)

    def set_out(bys):
        for by in bys:
            held[by] = spread_step([arrived[by]]) or [arrived[by]]

    held = {}
    arrived = {0: part_of(here // 2)}
    across = {0: part_of(here // 2 ^ 3)} if direct else {}

    ring_step(arrived, ring[:2], "weight_ring")
    arrived[0], x = after((arrived[0], x))
    key_blocks = [shift(k, "seq", by, "key_halo") for by in range(back, 0, -1)]
    x_mine, x_sent, k = x_halves_call(me, x, k, fsdp_count)
    key_blocks.append(k)
    probs, dv_blocks = probs_call(me, q, o, key_blocks)
    arrived, across, dv_blocks, x_mine, x_sent = after(
        (arrived, across, dv_blocks, x_mine, x_sent)
    )

    dv_back = [
        shift(dv_blocks[back - by], "seq", -by, "value_grad_halo") for by in range(1, back + 1)
    ]
    ring_step(arrived, ring[2:], "weight_ring")
    if direct:
        set_out(ring[:1])
    x_theirs = swap(x_sent, "x_core")
    acc, low = own_values_call(me, x_mine, x_theirs, down, up, w)
    held, late, dv_back, acc, low = after(
        (held, {by: arrived[by] for by in ring[2:]}, dv_back, acc, low)
    )
    arrived.update(late)

    if direct:
        set_out(ring[1:2])
        ring_step(across, ring[:1], "weight_ring_across")
    dv = dv_blocks[back]
    for block in dv_back:
        dv = dv + block.astype(F32)
    dv_mine = dv.astype(BF16)
    dv_theirs = swap(dv_mine, "value_grad_core")
    scale = 1.0 / (tokens * seq_count * fsdp_count)
    rank_grad, sums = adapter_grad_call(dv_mine, dv_theirs, up, low, x_mine, x_theirs, scale)
    across, held, sums = after((across, held, sums))

    steps = sum_steps(seq_count, fsdp_count)
    if direct:
        set_out(ring[2:])
        ring_step(across, ring[2:], "weight_ring_across")
        held = {
            by: held[by] + [across[by]] if by in across else spread_step(held[by]) for by in ring
        }
    else:
        set_out(ring)
    if len(steps) > 3:
        sums = sum_step(sums, steps.pop(0))
    held, acc, sums = after((held, acc, sums))
    while any(len(parts) < chips for parts in held.values()):
        held = after({by: spread_step(parts) for by, parts in held.items()})

    def arrays_of(parts):
        if pieces.by_parts:
            return parts
        return {by: natural_half(parts[by], pieces.order, here) for by in parts}

    if len(steps) > 2:
        sums = sum_step(sums, steps.pop(0))
    values, values_sent = more_values_call(
        me, x_mine, x_theirs, acc, arrays_of(held), pieces, True
    )

    values = (values + swap(values_sent, "values_core")).astype(BF16)
    values, dv_mine = after((values, dv_mine))
    value_blocks = [shift(values, "seq", by, "value_halo") for by in range(back, 0, -1)] + [values]
    while len(steps) > 1:
        sums = sum_step(sums, steps.pop(0))
    input_grad, input_grad_sent = input_grad_call(
        me, dv_mine, dv_theirs, rank_grad, down, w, arrays_of(held), pieces
    )
    value_blocks, sums, input_grad_sent = after((value_blocks, sums, input_grad_sent))

    total = sum_step(sums, steps[0], keep=True) if steps else sums.astype(F32)
    rotated_query_gradient, dk_blocks = scores_grad_call(probs, q, o, key_blocks, value_blocks)
    total, input_grad_sent, dk_blocks = after((total, input_grad_sent, dk_blocks))
    dk_back = [
        shift(dk_blocks[back - by], "seq", -by, "key_grad_halo") for by in range(1, back + 1)
    ]
    total_theirs = swap(total, "adapter_core")
    input_grad_theirs = swap(input_grad_sent, "input_grad_core")
    input_gradient = put_half_call(me, input_grad, input_grad_theirs, fsdp_count)
    down_gradient, up_gradient = join_call(me, total, total_theirs, fsdp_count, model)
    dk_back, input_gradient, down_gradient, up_gradient = after(
        (dk_back, input_gradient, down_gradient, up_gradient)
    )
    key_gradient = dk_blocks[back]
    for block in dk_back:
        key_gradient = key_gradient + block.astype(F32)
    return (
        input_gradient[None],
        rotated_query_gradient[None],
        key_gradient.astype(BF16)[None],
        down_gradient,
        up_gradient,
    )


def solution(mesh):
    placed = (
        P("fsdp", "seq", None),
        P("fsdp", "seq", None),
        P("fsdp", "seq", None),
        P("fsdp", "seq", None),
        P("fsdp", None),
        P(),
        P(),
        P("fsdp", None),
    )
    return jax.shard_map(
        body,
        mesh=mesh,
        in_specs=placed,
        out_specs=(
            P("fsdp", "seq", None),
            P("fsdp", "seq", None),
            P("fsdp", "seq", None),
            P(),
            P(),
        ),
        check_vma=False,
    )
```
